512 devices in a mesh: section: 32 (over z_lo, y, core), tp: 16 (over x, z_hi).
Axes of the slice: x: 4, y: 8, z: 8 (z_hi: 4, z_lo: 2; z = z_hi * 2 + z_lo), core: 2. Of those that a mesh axis runs over, the one named last changes fastest.
Arguments:
- block_weights: bfloat16 [32, 3072, 4, 2048], P(None, 'section', None, 'tp'), may hold values from -0.109375 to 0.109375
- modulation: float32 [32, 3, 3072], P('section'), may hold values from -4 to 4
- inflow: bfloat16 [32, 512, 3072], P('section', None, 'tp'), may hold values from -6 to 6
- stale_cache: bfloat16 [32, 2, 2048, 2048], P('section', None, None, 'tp'), may hold values from -120 to 120
- patch_index: int32 [32], P('section'), may hold values from 0 to 3
- assignment: int32 [32], replicated, may hold values from 0 to 31, each once
Outputs:
- outflow: bfloat16 [32, 512, 3072], P('section', None, 'tp')
The draws below stay inside these ranges and needn't reach their ends.
All inputs are finite; a program needn't handle non-finite values.
Results may differ from the reference program's by a relative error of at most 0.022.
Values may be sent and summed in bfloat16 or wider, within the bound.
A program may use at most 64 MiB of HBM per device.

```python
import jax
import jax.numpy as jnp
from jax import lax

D = 3072
HD = 128
HEADS = 16
INNER = 2048
PATCH = 512
SEQ = 2048
BLOCKS = 32
N_TP = 16


def draw_stale_cache(key, part):
    key = jax.random.fold_in(key, 11)
    first_key = jax.random.fold_in(key, 0)
    dims = (BLOCKS, 2, SEQ, INNER)
    scales = jnp.array([1.6, 3.0], jnp.float32).reshape(1, 2, 1, 1)
    drawn = jnp.clip(jax.random.normal(first_key, dims, jnp.float32), -6.0, 6.0)
    return (drawn * scales).astype(jnp.bfloat16)


def place_ends(entries, stream_key, smallest, high):
    longest = entries.shape.index(max(entries.shape))
    spots = []
    for shift in (0, 1):
        where = [jax.random.randint(jax.random.fold_in(stream_key, axis), (), 0, length) for axis, length in enumerate(entries.shape)]
        where[longest] = (where[longest] + shift) % entries.shape[longest]
        spots.append(tuple(where))
    return entries.at[spots[0]].set(smallest).at[spots[1]].set(high)


def level_of(own_key, extent, shards, low, top_value):
    level, own = 1.0, jax.random.fold_in(own_key, 6)
    for position, parts in shards:
        draws = jnp.exp(jax.random.uniform(jax.random.fold_in(own, position), (parts,), jnp.float32, low / len(shards), top_value / len(shards)))
        level = level * jnp.repeat(draws, extent[position] // parts).reshape([-1 if axis == position else 1 for axis in range(len(extent))])
    return level


def gaussian(own_key, shape, scale, bound, shards=(), kind=jnp.bfloat16):
    values = jax.random.normal(own_key, shape, jnp.float32) * scale
    if len(shards) > 0:
        values = level_of(own_key, shape, shards, -0.22, 0.18) * values
    return jnp.clip(values, min=-bound, max=bound).astype(kind)


def setup_inputs(seed: int = 0) -> dict:
    key_of = jax.random.split(jax.random.key(seed), 7)
    return {
        "block_weights": gaussian(key_of[0], (BLOCKS, D, 4, INNER), D ** -0.5, 0.109375, ((1, 32), (3, 16))),
        "modulation": gaussian(key_of[1], (BLOCKS, 3, D), 0.7, 4.0, ((0, 32),), jnp.float32),
        "inflow": gaussian(key_of[2], (BLOCKS, PATCH, D), 1.0, 6.0, ((0, 32), (2, 16))),
        "stale_cache": draw_stale_cache(jax.random.fold_in(key_of[6], 71), 0),
        "patch_index": place_ends(jax.random.randint(key_of[4], (BLOCKS,), 0, SEQ // PATCH), jax.random.fold_in(key_of[4], 1), 0, (SEQ // PATCH) - 1).astype(jnp.int32),
        "assignment": jax.random.permutation(key_of[5], BLOCKS).astype(jnp.int32),
    }


def run_section(block_weights, items):
    block, modulation_row, inflow_row, cache_row, patch_row = items
    weights = lax.dynamic_index_in_dim(block_weights, block, 0, keepdims=False)
    tokens = inflow_row.astype(jnp.float32)
    center = lax.optimization_barrier(jnp.mean(tokens, axis=1, keepdims=True))
    spread = lax.optimization_barrier(jnp.mean((tokens - center) ** 2, axis=1, keepdims=True))
    normed = (tokens - center) * lax.rsqrt(spread + 1e-06)
    normed = (normed * (1.0 + modulation_row[0]) + modulation_row[1]).astype(jnp.bfloat16)
    projected = jnp.dot(normed, weights[:, :3, :].reshape(D, 3 * INNER), preferred_element_type=jnp.float32)
    projected = projected.astype(jnp.bfloat16).reshape(PATCH, 3, HEADS, HD)
    start = (patch_row * PATCH).astype(jnp.int32)
    zero_index = jnp.zeros((), jnp.int32)
    keys_all = lax.dynamic_update_slice(cache_row[0], projected[:, 1].reshape(PATCH, INNER), (start, zero_index))
    values_all = lax.dynamic_update_slice(cache_row[1], projected[:, 2].reshape(PATCH, INNER), (start, zero_index))
    query = projected[:, 0].astype(jnp.float32)
    keys_heads = keys_all.reshape(SEQ, HEADS, HD).astype(jnp.float32)
    values_heads = values_all.reshape(SEQ, HEADS, HD).astype(jnp.float32)
    scores = jnp.einsum('phd,shd->hps', query, keys_heads) / jnp.sqrt(jnp.float32(HD))
    highest = lax.optimization_barrier(jnp.max(scores, axis=2, keepdims=True))
    expo = jnp.exp(scores - highest)
    probabilities = (expo / lax.optimization_barrier(jnp.sum(expo, axis=2, keepdims=True))).astype(jnp.bfloat16)
    attended = jnp.einsum('hps,shd->phd', probabilities.astype(jnp.float32), values_heads).astype(jnp.bfloat16)
    groups = attended.reshape(PATCH, N_TP, INNER // N_TP).astype(jnp.float32)
    output_proj = weights[:, 3, :].reshape(D, N_TP, INNER // N_TP).astype(jnp.float32)
    partials = jnp.einsum('pti,dti->tpd', groups, output_proj).astype(jnp.bfloat16)
    mixed = lax.optimization_barrier(jnp.sum(partials.astype(jnp.float32), axis=0))
    return (tokens + modulation_row[2] * mixed).astype(jnp.bfloat16)

def reference(block_weights, modulation, inflow, stale_cache, patch_index, assignment):
    section_ids = jnp.arange(BLOCKS, dtype=jnp.int32)
    owner_table = (assignment[None, :] == section_ids[:, None]).astype(jnp.int32)
    inverse = lax.optimization_barrier(jnp.sum(owner_table * section_ids[None, :], axis=1)).astype(jnp.int32)
    results = lax.map(lambda items: run_section(block_weights, items), (inverse, modulation, inflow, stale_cache, patch_index))
    return jnp.roll(results, 1, axis=0)
```

```python
import functools

import jax
import jax.numpy as jnp
from jax import lax
from jax.experimental import pallas as pl
from jax.experimental.pallas import tpu as pltpu
from jax.sharding import PartitionSpec as P

MESH = pl.DeviceIdType.MESH
F32 = jnp.float32
BF16 = jnp.bfloat16

HD = 128
D = 3072
PATCH = 512
SEQ = 2048
BLOCKS = 32
N_TP = 16
ROWS = D // BLOCKS
SHARE = D // N_TP
PACKED = PATCH + PATCH // 2
PER_X = D // 4
Q_STEP = 128


def peer_section(k, section):
    core = lax.rem(section, 2)
    y = lax.rem(section // 2, 8)
    z_lo = section // 16
    turn = k // 4
    flip = 3 - lax.rem(k, 4)
    half = (turn + 1) // 2
    dy = 4 + half * (1 - 2 * lax.rem(turn, 2))
    return (lax.rem(z_lo + flip // 2, 2) * 8 + lax.rem(y + dy, 8)) * 2 + lax.rem(core + lax.rem(flip, 2), 2)


def pack(value):
    tail = value[:, HD:SHARE]
    return value[:, :HD], jnp.concatenate([tail[: PATCH // 2], tail[PATCH // 2 :]], axis=1)


def kernel(
    inv_ref, patch_ref, w_hbm, mod_ref, x_hbm, stale_hbm, out_ref,
    w_v, x_v, stale_v, perm_v, send_w, wqkv, wo, xg, normed, q_v, k_v, v_v,
    o_stale, m_stale, l_stale, p_new, m_new, l_new, attg, part, rs_in, own, res, hand,
    sem_loc, ss_w, rs_w, rs_o, ss_own, ss_x, rs_x, ss_f, ss_a, rs_a, ss_r, rs_r, ss_h, rs_h,
):
    section = lax.axis_index("section")
    t = lax.axis_index("tp")
    x = t // 4
    zh = lax.rem(t, 4)
    y = lax.rem(section // 2, 8)
    xo = section // 8

    load_w = pltpu.make_async_copy(w_hbm, w_v, sem_loc.at[0])
    load_x = pltpu.make_async_copy(x_hbm, x_v, sem_loc.at[1])
    load_s = pltpu.make_async_copy(stale_hbm, stale_v, sem_loc.at[2])
    load_x.start()
    load_w.start()
    load_s.start()

    barrier = pltpu.get_barrier_semaphore()

    def greet(dev):
        pl.semaphore_signal(barrier, inc=1, device_id=dev, device_id_type=MESH)

    @pl.loop(0, BLOCKS - 1)
    def _(k):
        greet((peer_section(k, section), t))

    @pl.loop(0, BLOCKS)
    def _(k):
        greet((x * 8 + k // 4, lax.rem(k, 4) * 4 + zh))

    for d in range(1, 4):
        greet((section, lax.rem(x + d, 4) * 4 + zh))
        greet((section, x * 4 + lax.rem(zh + d, 4)))

    row = lax.broadcasted_iota(jnp.int32, (4 * ROWS, 4 * ROWS), 0)
    col = lax.broadcasted_iota(jnp.int32, (4 * ROWS, 4 * ROWS), 1)
    proj = (row >= ROWS).astype(jnp.int32) + (row >= 2 * ROWS).astype(jnp.int32) + (row >= 3 * ROWS).astype(jnp.int32)
    perm_v[...] = jnp.where(col == (row - proj * ROWS) * 4 + proj, 1.0, 0.0).astype(BF16)

    load_x.wait()
    head, tail = pack(x_v[...].astype(F32))
    xg[t, pl.ds(0, PATCH), :] = head.astype(BF16)
    xg[t, pl.ds(PATCH, PATCH // 2), :] = tail.astype(BF16)
    load_w.wait()

    pl.semaphore_wait(barrier, (BLOCKS - 1) + BLOCKS + 6)

    def send_x(slot, dev, sem):
        return pltpu.make_async_remote_copy(
            xg.at[slot], xg.at[slot], sem, rs_x.at[slot], device_id=dev, device_id_type=MESH
        )

    for d in range(1, 4):
        send_x(t, (section, x * 4 + lax.rem(zh + d, 4)), ss_x.at[d - 1]).start()
    for d in range(1, 4):
        send_x(t, (section, lax.rem(x + d, 4) * 4 + zh), ss_x.at[2 + d]).start()

    def sorted_rows(s):
        block = w_v[inv_ref[s]]
        return jnp.dot(perm_v[...], block, preferred_element_type=F32).astype(BF16)

    my_rows = pl.ds(pl.multiple_of(section * ROWS, ROWS), ROWS)

    def send_part(k, p):
        return pltpu.make_async_remote_copy(
            send_w.at[k, pl.ds(p * ROWS, ROWS)], wqkv.at[p, my_rows], ss_w.at[p], rs_w.at[p],
            device_id=(peer_section(k, section), t), device_id_type=MESH,
        )

    o_rows = pl.ds(pl.multiple_of(lax.rem(section, 8) * ROWS, ROWS), ROWS)
    o_group = lax.rem(section // 2, 4)

    def send_o(k, sem):
        return pltpu.make_async_remote_copy(
            send_w.at[k, pl.ds(3 * ROWS, ROWS)], wo.at[x, o_rows], sem, rs_o.at[o_group],
            device_id=(peer_section(k, section), xo * 4 + zh), device_id_type=MESH,
        )

    @pl.loop(0, BLOCKS - 1)
    def _(k):
        send_w[k] = sorted_rows(peer_section(k, section))
        send_part(k, 0).start()

    mine = sorted_rows(section)
    send_w[BLOCKS - 1] = mine
    for p in range(3):
        wqkv[p, my_rows, :] = mine[p * ROWS : (p + 1) * ROWS]

    for p in (1, 2):
        @pl.loop(0, BLOCKS - 1)
        def _(k):
            send_part(k, p).start()

    @pl.loop(0, BLOCKS - 1)
    def _(k):
        send_o(k, ss_w.at[3]).start()

    own_o = pltpu.make_async_copy(
        send_w.at[BLOCKS - 1, pl.ds(3 * ROWS, ROWS)], wo.at[x, o_rows], rs_o.at[o_group]
    )

    @pl.when(xo == x)
    def _():
        own_o.start()

    @pl.when(xo != x)
    def _():
        send_o(BLOCKS - 1, ss_own).start()

    for d in range(1, 4):
        slot = x * 4 + lax.rem(zh + d, 4)
        send_x(slot, (section, slot), ss_x.at[0]).wait_recv()
        for e in range(1, 4):
            dev = (section, lax.rem(x + e, 4) * 4 + zh)
            send_x(slot, dev, ss_f.at[3 * (d - 1) + e - 1]).start()

    for e in range(1, 4):
        for d in range(4):
            slot = lax.rem(x + e, 4) * 4 + lax.rem(zh + d, 4)
            send_x(slot, (section, slot), ss_x.at[0]).wait_recv()

    for h in range(2):
        @pl.loop(0, 8)
        def _(i):
            rows = pl.ds(pl.multiple_of(h * 256 + i * 32, 32), 32)
            tails = pl.ds(pl.multiple_of(PATCH + i * 32, 32), 32)
            pieces = []
            for u in range(N_TP):
                pieces.append(xg[u, rows, :].astype(F32))
                pieces.append(xg[u, tails, :].astype(F32)[:, 64 * h : 64 * h + 64])
            tokens = jnp.concatenate(pieces, axis=1)
            center = jnp.mean(tokens, axis=1, keepdims=True)
            shifted = tokens - center
            spread = jnp.mean(shifted * shifted, axis=1, keepdims=True)
            value = shifted * lax.rsqrt(spread + 1e-06)
            normed[rows, :] = (value * (1.0 + mod_ref[0:1, :]) + mod_ref[1:2, :]).astype(BF16)

    def wait_weights(p):
        view = wqkv.at[p, pl.ds(0, D - ROWS)]
        pltpu.make_async_copy(view, view, rs_w.at[p]).wait()

    def project(p, dst):
        @pl.loop(0, PATCH // Q_STEP)
        def _(i):
            rows = pl.ds(pl.multiple_of(i * Q_STEP, Q_STEP), Q_STEP)
            dst[rows, :] = jnp.dot(normed[rows, :], wqkv[p], preferred_element_type=F32).astype(BF16)

    NT = (((1,), (1,)), ((), ()))
    scaling = HD ** -0.5

    wait_weights(0)
    project(0, q_v)
    load_s.wait()
    patch = patch_ref[0]

    @pl.loop(0, PATCH // Q_STEP)
    def _(i):
        rows = pl.ds(pl.multiple_of(i * Q_STEP, Q_STEP), Q_STEP)
        query = q_v[rows, :]
        scores = []
        for j in range(1, 4):
            keys = stale_v[0, lax.rem(patch + j, 4)]
            scores.append(lax.dot_general(query, keys, NT, preferred_element_type=F32) * scaling)
        scores = jnp.concatenate(scores, axis=1)
        top = jnp.max(scores, axis=1, keepdims=True)
        expo = jnp.exp(scores - top)
        m_stale[rows, :] = jnp.broadcast_to(top, (Q_STEP, HD))
        l_stale[rows, :] = jnp.broadcast_to(jnp.sum(expo, axis=1, keepdims=True), (Q_STEP, HD))
        weights = expo.astype(BF16)
        total = jnp.zeros((Q_STEP, HD), F32)
        for j in range(1, 4):
            values = stale_v[1, lax.rem(patch + j, 4)]
            total += jnp.dot(weights[:, (j - 1) * PATCH : j * PATCH], values, preferred_element_type=F32)
        o_stale[rows, :] = total

    wait_weights(1)
    project(1, k_v)

    @pl.loop(0, PATCH // Q_STEP)
    def _(i):
        rows = pl.ds(pl.multiple_of(i * Q_STEP, Q_STEP), Q_STEP)
        scores = lax.dot_general(q_v[rows, :], k_v[...], NT, preferred_element_type=F32) * scaling
        top = jnp.max(scores, axis=1, keepdims=True)
        expo = jnp.exp(scores - top)
        l_part = jnp.broadcast_to(jnp.sum(expo, axis=1, keepdims=True), (Q_STEP, HD))
        top = jnp.broadcast_to(top, (Q_STEP, HD))
        high = jnp.maximum(top, m_stale[rows, :])
        a_new = jnp.exp(top - high)
        a_old = jnp.exp(m_stale[rows, :] - high)
        inverse = 1.0 / (a_new * l_part + a_old * l_stale[rows, :])
        m_new[rows, :] = a_new * inverse
        o_stale[rows, :] = o_stale[rows, :] * (a_old * inverse)
        p_new[rows, :] = expo.astype(BF16)

    wait_weights(2)
    project(2, v_v)

    @pl.loop(0, PATCH // Q_STEP)
    def _(i):
        rows = pl.ds(pl.multiple_of(i * Q_STEP, Q_STEP), Q_STEP)
        fresh = jnp.dot(p_new[rows, :], v_v[...], preferred_element_type=F32)
        attg[x, rows, :] = (o_stale[rows, :] + fresh * m_new[rows, :]).astype(BF16)

    def send_a(slot, e, sem):
        return pltpu.make_async_remote_copy(
            attg.at[slot], attg.at[slot], sem, rs_a.at[slot],
            device_id=(section, lax.rem(x + e, 4) * 4 + zh), device_id_type=MESH,
        )

    for e in range(1, 4):
        send_a(x, e, ss_a.at[e - 1]).start()
    for e in range(1, 4):
        send_a(lax.rem(x + e, 4), e, ss_a.at[e - 1]).wait_recv()

    def send_r(d):
        return pltpu.make_async_remote_copy(
            part.at[d - 1], rs_in.at[d - 1], ss_r.at[d - 1], rs_r.at[d - 1],
            device_id=(section, x * 4 + lax.rem(zh + d, 4)), device_id_type=MESH,
        )

    attended = jnp.concatenate([attg[i] for i in range(4)], axis=1)
    for d in (2, 1, 3, 0):
        group = lax.rem(zh + d, 4)
        features = pl.ds(pl.multiple_of(group * SHARE, SHARE), SHARE)
        view = wqkv.at[0, pl.ds(0, 8 * ROWS)]
        pltpu.make_async_copy(view, view, rs_o.at[group]).wait()
        weights = jnp.concatenate([wo[i, features, :] for i in range(4)], axis=1)
        partial_g = lax.dot_general(attended, weights, NT, preferred_element_type=F32)
        head, tail = pack(partial_g)
        if d > 0:
            part[d - 1, pl.ds(0, PATCH), :] = head.astype(BF16)
            part[d - 1, pl.ds(PATCH, PATCH // 2), :] = tail.astype(BF16)
            send_r(d).start()
        else:
            own[pl.ds(0, PATCH), :] = head
            own[pl.ds(PATCH, PATCH // 2), :] = tail

    gate = jnp.zeros((1, SHARE), F32)
    for u in range(N_TP):
        gate = jnp.where(t == u, mod_ref[2:3, u * SHARE : (u + 1) * SHARE], gate)
    gate_head = gate[:, :HD]
    gate_tail = jnp.concatenate([gate[:, HD:], gate[:, HD:]], axis=1)

    for d in (1, 2, 3):
        send_r(d).wait_recv()
    for start, size, g in ((0, PATCH, gate_head), (PATCH, PATCH // 2, gate_tail)):
        rows = pl.ds(start, size)
        mixed = own[rows, :] + rs_in[0, rows, :].astype(F32)
        mixed = mixed + rs_in[1, rows, :].astype(F32) + rs_in[2, rows, :].astype(F32)
        res[rows, :] = (xg[t, rows, :].astype(F32) + g * mixed).astype(BF16)

    handed = pltpu.make_async_remote_copy(
        res, hand, ss_h, rs_h, device_id=(lax.rem(section + 1, BLOCKS), t), device_id_type=MESH
    )
    handed.start()

    for p in range(4):
        view = wqkv.at[0, pl.ds(0, D - ROWS)]
        pltpu.make_async_copy(view, view, ss_w.at[p]).wait()

    @pl.when(xo != x)
    def _():
        send_o(BLOCKS - 1, ss_own).wait_send()

    for d in range(6):
        send_x(t, (section, t), ss_x.at[d]).wait_send()
    for d in range(9):
        send_x(t, (section, t), ss_f.at[d]).wait_send()
    for d in range(3):
        send_a(x, d + 1, ss_a.at[d]).wait_send()
        send_r(d + 1).wait_send()

    handed.wait()
    final_head = hand[pl.ds(0, PATCH), :].astype(F32)
    final_tail = hand[pl.ds(PATCH, PATCH // 2), :].astype(F32)
    final_tail = jnp.concatenate([final_tail[:, :64], final_tail[:, 64:]], axis=0)
    out_ref[...] = jnp.concatenate([final_head, final_tail], axis=1).astype(BF16)


def local(block_weights, modulation, inflow, stale_cache, patch_index, assignment):
    section_ids = jnp.arange(BLOCKS, dtype=jnp.int32)
    owner_table = (assignment[None, :] == section_ids[:, None]).astype(jnp.int32)
    inverse = jnp.sum(owner_table * section_ids[None, :], axis=1)

    vmem = pl.BlockSpec(memory_space=pltpu.VMEM)
    smem = pl.BlockSpec(memory_space=pltpu.SMEM)
    hbm = pl.BlockSpec(memory_space=pl.ANY)
    dma = pltpu.SemaphoreType.DMA
    result = pl.pallas_call(
        kernel,
        out_shape=jax.ShapeDtypeStruct((PATCH, SHARE), BF16),
        in_specs=[smem, smem, hbm, vmem, hbm, hbm],
        out_specs=vmem,
        scratch_shapes=[
            pltpu.VMEM((BLOCKS, 4 * ROWS, HD), BF16),
            pltpu.VMEM((PATCH, SHARE), BF16),
            pltpu.VMEM((2, 4, PATCH, HD), BF16),
            pltpu.VMEM((4 * ROWS, 4 * ROWS), BF16),
            pltpu.VMEM((BLOCKS, 4 * ROWS, HD), BF16),
            pltpu.VMEM((3, D, HD), BF16),
            pltpu.VMEM((4, PER_X, HD), BF16),
            pltpu.VMEM((N_TP, PACKED, HD), BF16),
            pltpu.VMEM((PATCH, D), BF16),
            pltpu.VMEM((PATCH, HD), BF16),
            pltpu.VMEM((PATCH, HD), BF16),
            pltpu.VMEM((PATCH, HD), BF16),
            pltpu.VMEM((PATCH, HD), F32),
            pltpu.VMEM((PATCH, HD), F32),
            pltpu.VMEM((PATCH, HD), F32),
            pltpu.VMEM((PATCH, PATCH), BF16),
            pltpu.VMEM((PATCH, HD), F32),
            pltpu.VMEM((PATCH, HD), F32),
            pltpu.VMEM((4, PATCH, HD), BF16),
            pltpu.VMEM((3, PACKED, HD), BF16),
            pltpu.VMEM((3, PACKED, HD), BF16),
            pltpu.VMEM((PACKED, HD), F32),
            pltpu.VMEM((PACKED, HD), BF16),
            pltpu.VMEM((PACKED, HD), BF16),
            dma((3,)), dma((4,)), dma((3,)), dma((4,)), dma,
            dma((6,)), dma((N_TP,)), dma((9,)), dma((3,)), dma((4,)), dma((3,)), dma((3,)), dma, dma,
        ],
        compiler_params=pltpu.CompilerParams(
            collective_id=0, has_side_effects=True, vmem_limit_bytes=48 * 2**20
        ),
    )(
        inverse,
        patch_index,
        block_weights.reshape(BLOCKS, 4 * ROWS, HD),
        modulation.reshape(3, D),
        inflow.reshape(PATCH, SHARE),
        stale_cache.reshape(2, 4, PATCH, HD),
    )
    return result[None]


def solution(mesh):
    placed = (
        P(None, "section", None, "tp"),
        P("section", None, None),
        P("section", None, "tp"),
        P("section", None, None, "tp"),
        P("section"),
        P(),
    )
    return jax.shard_map(
        local, mesh=mesh, in_specs=placed, out_specs=P("section", None, "tp"), check_vma=False
    )
```

```python
import functools

import jax
import jax.numpy as jnp
from jax import lax
from jax.experimental import pallas as pl
from jax.experimental.pallas import tpu as pltpu
from jax.sharding import PartitionSpec as P

MESH = pl.DeviceIdType.MESH
F32 = jnp.float32
BF16 = jnp.bfloat16

HD = 128
D = 3072
PATCH = 512
SEQ = 2048
BLOCKS = 32
N_TP = 16
ROWS = D // BLOCKS
SHARE = D // N_TP
HALF = SHARE // 2
PER_X = D // 4
Q_STEP = 128


def peer_section(k, section):
    core = lax.rem(section, 2)
    y = lax.rem(section // 2, 8)
    z_lo = section // 16
    turn = k // 4
    flip = 3 - lax.rem(k, 4)
    half = (turn + 1) // 2
    dy = 4 + half * (1 - 2 * lax.rem(turn, 2))
    return (lax.rem(z_lo + flip // 2, 2) * 8 + lax.rem(y + dy, 8)) * 2 + lax.rem(core + lax.rem(flip, 2), 2)


def kernel(
    assign_ref, patch_ref, w_hbm, mod_hbm, x_hbm, stale_hbm, out_ref,
    w_v, mod_v, columns, stale_v, perm_v, send_w, wqkv, wo, xg, normed, q_v, k_v, v_v,
    o_stale, m_stale, l_stale, p_new, m_new, attg, stats, norm_v, quarters, part, far_in, near_in, res,
    sem_loc, ss_w, rs_w, rs_o, ss_own, ss_x, rs_x, ss_f, ss_a, rs_a, ss_r, rs_r, ss_h, rs_h,
):
    section = lax.axis_index("section")
    t = lax.axis_index("tp")
    x = t // 4
    zh = lax.rem(t, 4)
    y = lax.rem(section // 2, 8)
    xo = section // 8

    load_w = pltpu.make_async_copy(w_hbm, w_v, sem_loc.at[0])
    my_features = pl.ds(pl.multiple_of(t * SHARE, SHARE), SHARE)
    load_x = pltpu.make_async_copy(x_hbm, xg.at[my_features], sem_loc.at[1])
    load_s = pltpu.make_async_copy(stale_hbm, stale_v, sem_loc.at[2])
    load_m = pltpu.make_async_copy(mod_hbm, mod_v, sem_loc.at[3])
    load_x.start()
    load_w.start()
    load_m.start()
    load_s.start()

    barrier = pltpu.get_barrier_semaphore()

    def greet(dev):
        pl.semaphore_signal(barrier, inc=1, device_id=dev, device_id_type=MESH)

    @pl.loop(0, BLOCKS - 1)
    def _(k):
        greet((peer_section(k, section), t))

    @pl.loop(0, BLOCKS)
    def _(k):
        greet((x * 8 + k // 4, lax.rem(k, 4) * 4 + zh))

    for d in range(1, 4):
        greet((section, lax.rem(x + d, 4) * 4 + zh))
        greet((section, x * 4 + lax.rem(zh + d, 4)))

    row = lax.broadcasted_iota(jnp.int32, (4 * ROWS, 4 * ROWS), 0)
    col = lax.broadcasted_iota(jnp.int32, (4 * ROWS, 4 * ROWS), 1)
    proj = (row >= ROWS).astype(jnp.int32) + (row >= 2 * ROWS).astype(jnp.int32) + (row >= 3 * ROWS).astype(jnp.int32)
    perm_v[...] = jnp.where(col == (row - proj * ROWS) * 4 + proj, 1.0, 0.0).astype(BF16)

    load_x.wait()
    load_w.wait()

    pl.semaphore_wait(barrier, (BLOCKS - 1) + BLOCKS + 6)

    def send_x(slot, dev, sem):
        rows = pl.ds(pl.multiple_of(slot * SHARE, SHARE), SHARE)
        return pltpu.make_async_remote_copy(
            xg.at[rows], xg.at[rows], sem, rs_x.at[slot], device_id=dev, device_id_type=MESH
        )

    for d in range(1, 4):
        send_x(t, (section, x * 4 + lax.rem(zh + d, 4)), ss_x.at[d - 1]).start()
    for d in range(1, 4):
        send_x(t, (section, lax.rem(x + d, 4) * 4 + zh), ss_x.at[2 + d]).start()

    def sorted_rows(s):
        owner = jnp.int32(0)
        for b in range(1, BLOCKS):
            owner = jnp.where(assign_ref[b] == s, b, owner)
        block = w_v[owner]
        return jnp.dot(perm_v[...], block, preferred_element_type=F32).astype(BF16)

    my_rows = pl.ds(pl.multiple_of(section * ROWS, ROWS), ROWS)

    def send_part(k, p):
        return pltpu.make_async_remote_copy(
            send_w.at[k, pl.ds(p * ROWS, ROWS)], wqkv.at[p, my_rows], ss_w.at[p], rs_w.at[p],
            device_id=(peer_section(k, section), t), device_id_type=MESH,
        )

    o_rows = pl.ds(pl.multiple_of(lax.rem(section, 8) * ROWS, ROWS), ROWS)
    o_group = lax.rem(section // 2, 4)

    def send_o(k, sem):
        return pltpu.make_async_remote_copy(
            send_w.at[k, pl.ds(3 * ROWS, ROWS)], wo.at[x, o_rows], sem, rs_o.at[o_group],
            device_id=(peer_section(k, section), xo * 4 + zh), device_id_type=MESH,
        )

    @pl.loop(0, BLOCKS - 1)
    def _(k):
        send_w[k] = sorted_rows(peer_section(k, section))
        send_part(k, 0).start()

    mine = sorted_rows(section)
    send_w[BLOCKS - 1] = mine
    for p in range(3):
        wqkv[p, my_rows, :] = mine[p * ROWS : (p + 1) * ROWS]

    for p in (1, 2):
        @pl.loop(0, BLOCKS - 1)
        def _(k):
            send_part(k, p).start()

    @pl.loop(0, BLOCKS - 1)
    def _(k):
        send_o(k, ss_w.at[3]).start()

    own_o = pltpu.make_async_copy(
        send_w.at[BLOCKS - 1, pl.ds(3 * ROWS, ROWS)], wo.at[x, o_rows], rs_o.at[o_group]
    )

    @pl.when(xo == x)
    def _():
        own_o.start()

    @pl.when(xo != x)
    def _():
        send_o(BLOCKS - 1, ss_own).start()

    load_m.wait()

    @pl.loop(0, D // HD)
    def _(c):
        features = pl.ds(pl.multiple_of(c * HD, HD), HD)
        for p in range(3):
            columns[p, features, :] = jnp.broadcast_to(mod_v[p, :, features], (HD, HD)).T

    def take_stats(slot):
        rows = pl.ds(pl.multiple_of(slot * SHARE, SHARE), SHARE)
        tokens = xg[rows, :].astype(F32)
        mean = jnp.sum(jnp.sum(tokens.reshape(SHARE // 8, 8, PATCH), axis=0), axis=0, keepdims=True) / SHARE
        shifted = tokens - mean
        shifted = shifted * shifted
        moment = jnp.sum(jnp.sum(shifted.reshape(SHARE // 8, 8, PATCH), axis=0), axis=0, keepdims=True)
        stats[slot] = jnp.concatenate([mean, moment], axis=0)

    @pl.loop(1, 4)
    def _(d):
        slot = x * 4 + lax.rem(zh + d, 4)
        send_x(slot, (section, slot), ss_x.at[0]).wait_recv()
        for e in range(1, 4):
            dev = (section, lax.rem(x + e, 4) * 4 + zh)
            send_x(slot, dev, ss_f.at[3 * (d - 1) + e - 1]).start()

    @pl.loop(0, 4)
    def _(d):
        take_stats(x * 4 + lax.rem(zh + d, 4))

    @pl.loop(0, 12)
    def _(i):
        slot = lax.rem(x + 1 + lax.rem(i, 3), 4) * 4 + lax.rem(zh + i // 3, 4)
        send_x(slot, (section, slot), ss_x.at[0]).wait_recv()
        take_stats(slot)

    means = stats[:, 0, :]
    center = jnp.sum(means, axis=0, keepdims=True) / N_TP
    means = means - center
    moment = jnp.sum(stats[:, 1, :] + SHARE * means * means, axis=0, keepdims=True)
    inverse = lax.rsqrt(moment / D + 1e-06)
    norm_v[0:1, :] = center
    norm_v[1:2, :] = inverse

    @pl.loop(0, D // HD)
    def _(c):
        features = pl.ds(pl.multiple_of(c * HD, HD), HD)
        scale = 1.0 + columns[0, features, :]
        shift = columns[1, features, :]
        for i in range(PATCH // HD):
            tokens = pl.ds(i * HD, HD)
            value = (xg[features, tokens].astype(F32) - norm_v[0:1, tokens]) * norm_v[1:2, tokens]
            normed[tokens, features] = (value * scale + shift).T.astype(BF16)

    def wait_weights(p):
        view = wqkv.at[p, pl.ds(0, D - ROWS)]
        pltpu.make_async_copy(view, view, rs_w.at[p]).wait()

    def project(p, dst):
        @pl.loop(0, PATCH // Q_STEP)
        def _(i):
            rows = pl.ds(pl.multiple_of(i * Q_STEP, Q_STEP), Q_STEP)
            dst[rows, :] = jnp.dot(normed[rows, :], wqkv[p], preferred_element_type=F32).astype(BF16)

    NT = (((1,), (1,)), ((), ()))
    scaling = HD ** -0.5

    wait_weights(0)
    project(0, q_v)
    load_s.wait()
    patch = patch_ref[0]

    @pl.loop(0, PATCH // Q_STEP)
    def _(i):
        rows = pl.ds(pl.multiple_of(i * Q_STEP, Q_STEP), Q_STEP)
        query = q_v[rows, :]
        scores = []
        for j in range(1, 4):
            keys = stale_v[0, lax.rem(patch + j, 4)]
            scores.append(lax.dot_general(query, keys, NT, preferred_element_type=F32) * scaling)
        scores = jnp.concatenate(scores, axis=1)
        top = jnp.max(scores, axis=1, keepdims=True)
        expo = jnp.exp(scores - top)
        m_stale[rows, :] = jnp.broadcast_to(top, (Q_STEP, HD))
        l_stale[rows, :] = jnp.broadcast_to(jnp.sum(expo, axis=1, keepdims=True), (Q_STEP, HD))
        weights = expo.astype(BF16)
        total = jnp.zeros((Q_STEP, HD), F32)
        for j in range(1, 4):
            values = stale_v[1, lax.rem(patch + j, 4)]
            total += jnp.dot(weights[:, (j - 1) * PATCH : j * PATCH], values, preferred_element_type=F32)
        o_stale[rows, :] = total

    wait_weights(1)
    project(1, k_v)

    @pl.loop(0, PATCH // Q_STEP)
    def _(i):
        rows = pl.ds(pl.multiple_of(i * Q_STEP, Q_STEP), Q_STEP)
        scores = lax.dot_general(q_v[rows, :], k_v[...], NT, preferred_element_type=F32) * scaling
        top = jnp.max(scores, axis=1, keepdims=True)
        expo = jnp.exp(scores - top)
        l_part = jnp.broadcast_to(jnp.sum(expo, axis=1, keepdims=True), (Q_STEP, HD))
        top = jnp.broadcast_to(top, (Q_STEP, HD))
        high = jnp.maximum(top, m_stale[rows, :])
        a_new = jnp.exp(top - high)
        a_old = jnp.exp(m_stale[rows, :] - high)
        inverse = 1.0 / (a_new * l_part + a_old * l_stale[rows, :])
        m_new[rows, :] = a_new * inverse
        o_stale[rows, :] = o_stale[rows, :] * (a_old * inverse)
        p_new[rows, :] = expo.astype(BF16)

    wait_weights(2)
    project(2, v_v)

    @pl.loop(0, PATCH // Q_STEP)
    def _(i):
        rows = pl.ds(pl.multiple_of(i * Q_STEP, Q_STEP), Q_STEP)
        fresh = jnp.dot(p_new[rows, :], v_v[...], preferred_element_type=F32)
        attg[x, rows, :] = (o_stale[rows, :] + fresh * m_new[rows, :]).astype(BF16)

    def send_a(slot, e, sem):
        return pltpu.make_async_remote_copy(
            attg.at[slot], attg.at[slot], sem, rs_a.at[slot],
            device_id=(section, lax.rem(x + e, 4) * 4 + zh), device_id_type=MESH,
        )

    for e in range(1, 4):
        send_a(x, e, ss_a.at[e - 1]).start()
    for e in range(1, 4):
        send_a(lax.rem(x + e, 4), e, ss_a.at[e - 1]).wait_recv()

    def along(sign):
        return (section, x * 4 + lax.rem(zh + 4 + sign, 4))

    def remote(src, dst, k, sign):
        return pltpu.make_async_remote_copy(
            src, dst, ss_r.at[k], rs_r.at[k], device_id=along(sign), device_id_type=MESH
        )

    low, high = pl.ds(0, HALF), pl.ds(HALF, HALF)
    far_up = remote(part.at[0, low], far_in.at[0], 0, 1)
    far_down = remote(part.at[0, high], far_in.at[1], 1, -1)
    plain_up = remote(part.at[1, high], near_in.at[0, high], 2, 1)
    plain_down = remote(part.at[2, low], near_in.at[1, low], 3, -1)
    sum_up = remote(part.at[1, low], near_in.at[0, low], 4, 1)
    sum_down = remote(part.at[2, high], near_in.at[1, high], 5, -1)

    at = lax.rem(y, 4)
    rising = 228 - 3 * at - 84 * at * (at - 1) + 52 * at * (at - 1) * (at - 2)
    falling = 27 + 48 * at + 33 * ((at * (at - 1)) // 2) - 7 * at * (at - 1) * (at - 2)
    other = lax.rem(y // 4 + lax.rem(x, 2), 2)

    def quarter(i, code):
        group = lax.rem(code, 4)
        step = lax.rem(group - zh + 4, 4)
        features = pl.ds(pl.multiple_of(group * SHARE, SHARE), SHARE)
        view = wqkv.at[0, pl.ds(0, 8 * ROWS)]
        pltpu.make_async_copy(view, view, rs_o.at[group]).wait()
        attended = jnp.concatenate([attg[j] for j in range(4)], axis=1)
        weights = jnp.concatenate([wo[j, features, :] for j in range(4)], axis=1)
        quarters[step] = lax.dot_general(weights, attended, NT, preferred_element_type=F32)

        @pl.when(step == 2)
        def _():
            part[0] = quarters[2].astype(BF16)
            far_up.start()
            far_down.start()

        @pl.when(step == 1)
        def _():
            part[1, high, :] = quarters[1, high, :].astype(BF16)
            plain_up.start()

        @pl.when(step == 3)
        def _():
            part[2, low, :] = quarters[3, low, :].astype(BF16)
            plain_down.start()

        return code // 4

    lax.fori_loop(0, 4, quarter, other * rising + (1 - other) * falling)

    far_up.wait_recv()
    part[1, low, :] = (quarters[1, low, :] + far_in[0].astype(F32)).astype(BF16)
    sum_up.start()
    far_down.wait_recv()
    part[2, high, :] = (quarters[3, high, :] + far_in[1].astype(F32)).astype(BF16)
    sum_down.start()

    def hand(k):
        rows = pl.ds(k * HALF, HALF)
        return pltpu.make_async_remote_copy(
            res.at[rows], out_ref.at[rows], ss_h.at[k], rs_h.at[k],
            device_id=(lax.rem(section + 1, BLOCKS), t), device_id_type=MESH,
        )

    for k, first, second in ((0, plain_down, sum_up), (1, plain_up, sum_down)):
        first.wait_recv()
        second.wait_recv()
        rows = pl.ds(k * HALF, HALF)
        mine_rows = pl.ds(pl.multiple_of(t * SHARE + k * HALF, HALF), HALF)
        gate = columns[2, mine_rows, :]
        for i in range(PATCH // HD):
            tokens = pl.ds(i * HD, HD)
            mixed = quarters[0, rows, tokens] + near_in[0, rows, tokens].astype(F32) + near_in[1, rows, tokens].astype(F32)
            res[rows, tokens] = (xg[mine_rows, tokens].astype(F32) + gate * mixed).astype(BF16)
        hand(k).start()

    for p in range(4):
        view = wqkv.at[0, pl.ds(0, D - ROWS)]
        pltpu.make_async_copy(view, view, ss_w.at[p]).wait()

    @pl.when(xo != x)
    def _():
        send_o(BLOCKS - 1, ss_own).wait_send()

    for d in range(6):
        send_x(t, (section, t), ss_x.at[d]).wait_send()
    for d in range(9):
        send_x(t, (section, t), ss_f.at[d]).wait_send()
    for d in range(3):
        send_a(x, d + 1, ss_a.at[d]).wait_send()
    for copy in (far_up, far_down, plain_up, plain_down, sum_up, sum_down):
        copy.wait_send()
    for k in range(2):
        hand(k).wait()


def local(block_weights, modulation, inflow, stale_cache, patch_index, assignment):
    vmem = pl.BlockSpec(memory_space=pltpu.VMEM)
    smem = pl.BlockSpec(memory_space=pltpu.SMEM)
    hbm = pl.BlockSpec(memory_space=pltpu.HBM)
    dma = pltpu.SemaphoreType.DMA
    result = pl.pallas_call(
        kernel,
        out_shape=jax.ShapeDtypeStruct((SHARE, PATCH), BF16),
        in_specs=[smem, smem, hbm, hbm, hbm, hbm],
        out_specs=vmem,
        scratch_shapes=[
            pltpu.VMEM((BLOCKS, 4 * ROWS, HD), BF16),
            pltpu.VMEM((3, 1, D), F32),
            pltpu.VMEM((3, D, HD), F32),
            pltpu.VMEM((2, 4, PATCH, HD), BF16),
            pltpu.VMEM((4 * ROWS, 4 * ROWS), BF16),
            pltpu.VMEM((BLOCKS, 4 * ROWS, HD), BF16),
            pltpu.VMEM((3, D, HD), BF16),
            pltpu.VMEM((4, PER_X, HD), BF16),
            pltpu.VMEM((D, PATCH), BF16),
            pltpu.VMEM((PATCH, D), BF16),
            pltpu.VMEM((PATCH, HD), BF16),
            pltpu.VMEM((PATCH, HD), BF16),
            pltpu.VMEM((PATCH, HD), BF16),
            pltpu.VMEM((PATCH, HD), F32),
            pltpu.VMEM((PATCH, HD), F32),
            pltpu.VMEM((PATCH, HD), F32),
            pltpu.VMEM((PATCH, PATCH), BF16),
            pltpu.VMEM((PATCH, HD), F32),
            pltpu.VMEM((4, PATCH, HD), BF16),
            pltpu.VMEM((N_TP, 2, PATCH), F32),
            pltpu.VMEM((8, PATCH), F32),
            pltpu.VMEM((4, SHARE, PATCH), F32),
            pltpu.VMEM((3, SHARE, PATCH), BF16),
            pltpu.VMEM((2, HALF, PATCH), BF16),
            pltpu.VMEM((2, SHARE, PATCH), BF16),
            pltpu.VMEM((SHARE, PATCH), BF16),
            dma((4,)), dma((4,)), dma((3,)), dma((4,)), dma,
            dma((6,)), dma((N_TP,)), dma((9,)), dma((3,)), dma((4,)), dma((6,)), dma((6,)), dma((2,)), dma((2,)),
        ],
        compiler_params=pltpu.CompilerParams(
            collective_id=0, has_side_effects=True, vmem_limit_bytes=60 * 2**20
        ),
    )(
        assignment,
        patch_index,
        block_weights.reshape(BLOCKS, 4 * ROWS, HD),
        modulation.transpose(1, 0, 2),
        inflow[0].T,
        stale_cache.reshape(2, 4, PATCH, HD),
    )
    return result.T[None]


def solution(mesh):
    placed = (
        P(None, "section", None, "tp"),
        P("section", None, None),
        P("section", None, "tp"),
        P("section", None, None, "tp"),
        P("section"),
        P(),
    )
    return jax.shard_map(
        local, mesh=mesh, in_specs=placed, out_specs=P("section", None, "tp"), check_vma=False
    )
```

```python
import functools

import jax
import jax.numpy as jnp
from jax import lax
from jax.experimental import pallas as pl
from jax.experimental.pallas import tpu as pltpu
from jax.sharding import PartitionSpec as P

MESH = pl.DeviceIdType.MESH
F32 = jnp.float32
BF16 = jnp.bfloat16

HD = 128
D = 3072
PATCH = 512
SEQ = 2048
BLOCKS = 32
N_TP = 16
ROWS = D // BLOCKS
SHARE = D // N_TP
HALF = SHARE // 2
CHUNKS = PATCH // HD
PER_X = D // 4
Q_STEP = 128


def peer_section(k, section):
    core = lax.rem(section, 2)
    y = lax.rem(section // 2, 8)
    z_lo = section // 16
    turn = k // 4
    flip = 3 - lax.rem(k, 4)
    half = (turn + 1) // 2
    dy = 4 + half * (1 - 2 * lax.rem(turn, 2))
    return (lax.rem(z_lo + flip // 2, 2) * 8 + lax.rem(y + dy, 8)) * 2 + lax.rem(core + lax.rem(flip, 2), 2)


def kernel(
    assign_ref, patch_ref, w_hbm, mod_hbm, x_hbm, stale_hbm, out_ref,
    w_v, mod_v, columns, stale_v, perm_v, send_w, wqkv, wo, xg, normed, q_v, k_v, v_v,
    o_stale, m_stale, l_stale, p_new, m_new, attg, stats, norm_v, quarters, part, far_in, near_in, res,
    sem_loc, ss_w, rs_w, rs_o, ss_own, ss_x, rs_x, ss_f, ss_a, rs_a, ss_r, rs_r, ss_h, rs_h,
):
    section = lax.axis_index("section")
    t = lax.axis_index("tp")
    x = t // 4
    zh = lax.rem(t, 4)
    y = lax.rem(section // 2, 8)
    xo = section // 8

    load_w = pltpu.make_async_copy(w_hbm, w_v, sem_loc.at[0])
    my_features = pl.ds(pl.multiple_of(t * SHARE, SHARE), SHARE)
    load_x = pltpu.make_async_copy(x_hbm, xg.at[my_features], sem_loc.at[1])
    load_s = pltpu.make_async_copy(stale_hbm, stale_v, sem_loc.at[2])
    load_m = pltpu.make_async_copy(mod_hbm, mod_v, sem_loc.at[3])
    load_x.start()
    load_w.start()
    load_m.start()
    load_s.start()

    barrier = pltpu.get_barrier_semaphore()

    def greet(dev):
        pl.semaphore_signal(barrier, inc=1, device_id=dev, device_id_type=MESH)

    @pl.loop(0, BLOCKS - 1)
    def _(k):
        greet((peer_section(k, section), t))

    @pl.loop(0, BLOCKS)
    def _(k):
        greet((x * 8 + k // 4, lax.rem(k, 4) * 4 + zh))

    for d in range(1, 4):
        greet((section, lax.rem(x + d, 4) * 4 + zh))
        greet((section, x * 4 + lax.rem(zh + d, 4)))

    row = lax.broadcasted_iota(jnp.int32, (4 * ROWS, 4 * ROWS), 0)
    col = lax.broadcasted_iota(jnp.int32, (4 * ROWS, 4 * ROWS), 1)
    proj = (row >= ROWS).astype(jnp.int32) + (row >= 2 * ROWS).astype(jnp.int32) + (row >= 3 * ROWS).astype(jnp.int32)
    perm_v[...] = jnp.where(col == (row - proj * ROWS) * 4 + proj, 1.0, 0.0).astype(BF16)

    load_x.wait()
    load_w.wait()

    pl.semaphore_wait(barrier, (BLOCKS - 1) + BLOCKS + 6)

    def send_x(slot, dev, sem):
        rows = pl.ds(pl.multiple_of(slot * SHARE, SHARE), SHARE)
        return pltpu.make_async_remote_copy(
            xg.at[rows], xg.at[rows], sem, rs_x.at[slot], device_id=dev, device_id_type=MESH
        )

    def send_z(d):
        return send_x(t, (section, x * 4 + lax.rem(zh + d, 4)), ss_x.at[d - 1])

    def pass_on(d):
        slot = x * 4 + lax.rem(zh + d, 4)
        send_x(slot, (section, slot), ss_x.at[0]).wait_recv()
        for e in range(1, 4):
            dev = (section, lax.rem(x + e, 4) * 4 + zh)
            send_x(slot, dev, ss_f.at[3 * (d - 1) + e - 1]).start()

    send_z(1).start()
    send_z(3).start()
    send_z(2).start()
    for d in range(1, 4):
        send_x(t, (section, lax.rem(x + d, 4) * 4 + zh), ss_x.at[2 + d]).start()

    def block_of(s):
        owner = jnp.int32(0)
        for b in range(1, BLOCKS):
            owner = jnp.where(assign_ref[b] == s, b, owner)
        return w_v[owner]

    my_rows = pl.ds(pl.multiple_of(section * ROWS, ROWS), ROWS)

    def send_part(k, p):
        return pltpu.make_async_remote_copy(
            send_w.at[k, pl.ds(p * ROWS, ROWS)], wqkv.at[p, my_rows], ss_w.at[p], rs_w.at[p],
            device_id=(peer_section(k, section), t), device_id_type=MESH,
        )

    o_rows = pl.ds(pl.multiple_of(lax.rem(section, 8) * ROWS, ROWS), ROWS)
    o_group = lax.rem(section // 2, 4)

    def send_o(k, sem):
        return pltpu.make_async_remote_copy(
            send_w.at[k, pl.ds(3 * ROWS, ROWS)], wo.at[x, o_rows], sem, rs_o.at[o_group],
            device_id=(peer_section(k, section), xo * 4 + zh), device_id_type=MESH,
        )

    @pl.loop(0, BLOCKS // 4)
    def _(g):
        blocks = jnp.concatenate([block_of(peer_section(4 * g + i, section)) for i in range(4)], axis=1)
        ordered = jnp.dot(perm_v[...], blocks, preferred_element_type=F32).astype(BF16)
        for i in range(4):
            send_w[4 * g + i] = ordered[:, i * HD : (i + 1) * HD]
        for i in range(3):
            send_part(4 * g + i, 0).start()

        @pl.when(g < BLOCKS // 4 - 1)
        def _():
            send_part(4 * g + 3, 0).start()

    for p in range(3):
        wqkv[p, my_rows, :] = send_w[BLOCKS - 1, pl.ds(p * ROWS, ROWS), :]
    pass_on(1)
    pass_on(3)

    @pl.loop(0, BLOCKS - 1)
    def _(k):
        send_part(k, 1).start()

    pass_on(2)

    @pl.loop(0, BLOCKS - 1)
    def _(k):
        send_part(k, 2).start()

    @pl.loop(0, BLOCKS - 1)
    def _(k):
        send_o(k, ss_w.at[3]).start()

    own_o = pltpu.make_async_copy(
        send_w.at[BLOCKS - 1, pl.ds(3 * ROWS, ROWS)], wo.at[x, o_rows], rs_o.at[o_group]
    )

    @pl.when(xo == x)
    def _():
        own_o.start()

    @pl.when(xo != x)
    def _():
        send_o(BLOCKS - 1, ss_own).start()

    load_m.wait()

    @pl.loop(0, D // HD)
    def _(c):
        features = pl.ds(pl.multiple_of(c * HD, HD), HD)
        for p in range(3):
            columns[p, features, :] = jnp.broadcast_to(mod_v[p, :, features], (HD, HD)).T

    def take_stats(slot):
        rows = pl.ds(pl.multiple_of(slot * SHARE, SHARE), SHARE)
        tokens = xg[rows, :].astype(F32)
        mean = jnp.sum(jnp.sum(tokens.reshape(SHARE // 8, 8, PATCH), axis=0), axis=0, keepdims=True) / SHARE
        shifted = tokens - mean
        shifted = shifted * shifted
        moment = jnp.sum(jnp.sum(shifted.reshape(SHARE // 8, 8, PATCH), axis=0), axis=0, keepdims=True)
        stats[slot] = jnp.concatenate([mean, moment], axis=0)

    @pl.loop(0, 4)
    def _(d):
        take_stats(x * 4 + lax.rem(zh + d, 4))

    @pl.loop(0, 12)
    def _(i):
        slot = lax.rem(x + 1 + lax.rem(i, 3), 4) * 4 + lax.rem(zh + i // 3, 4)
        send_x(slot, (section, slot), ss_x.at[0]).wait_recv()
        take_stats(slot)

    means = stats[:, 0, :]
    center = jnp.sum(means, axis=0, keepdims=True) / N_TP
    means = means - center
    moment = jnp.sum(stats[:, 1, :] + SHARE * means * means, axis=0, keepdims=True)
    inverse = lax.rsqrt(moment / D + 1e-06)
    norm_v[0:1, :] = center
    norm_v[1:2, :] = inverse

    @pl.loop(0, D // HD)
    def _(c):
        features = pl.ds(pl.multiple_of(c * HD, HD), HD)
        scale = 1.0 + columns[0, features, :]
        shift = columns[1, features, :]
        for i in range(PATCH // HD):
            tokens = pl.ds(i * HD, HD)
            value = (xg[features, tokens].astype(F32) - norm_v[0:1, tokens]) * norm_v[1:2, tokens]
            normed[tokens, features] = (value * scale + shift).T.astype(BF16)

    def wait_weights(p):
        view = wqkv.at[p, pl.ds(0, D - ROWS)]
        pltpu.make_async_copy(view, view, rs_w.at[p]).wait()

    def project(p, dst):
        @pl.loop(0, PATCH // Q_STEP)
        def _(i):
            rows = pl.ds(pl.multiple_of(i * Q_STEP, Q_STEP), Q_STEP)
            dst[rows, :] = jnp.dot(normed[rows, :], wqkv[p], preferred_element_type=F32).astype(BF16)

    NT = (((1,), (1,)), ((), ()))
    scaling = HD ** -0.5

    wait_weights(0)
    project(0, q_v)
    load_s.wait()
    patch = patch_ref[0]

    @pl.loop(0, PATCH // Q_STEP)
    def _(i):
        rows = pl.ds(pl.multiple_of(i * Q_STEP, Q_STEP), Q_STEP)
        query = q_v[rows, :]
        scores = []
        for j in range(1, 4):
            keys = stale_v[0, lax.rem(patch + j, 4)]
            scores.append(lax.dot_general(query, keys, NT, preferred_element_type=F32) * scaling)
        scores = jnp.concatenate(scores, axis=1)
        top = jnp.max(scores, axis=1, keepdims=True)
        expo = jnp.exp(scores - top)
        m_stale[rows, :] = jnp.broadcast_to(top, (Q_STEP, HD))
        l_stale[rows, :] = jnp.broadcast_to(jnp.sum(expo, axis=1, keepdims=True), (Q_STEP, HD))
        weights = expo.astype(BF16)
        total = jnp.zeros((Q_STEP, HD), F32)
        for j in range(1, 4):
            values = stale_v[1, lax.rem(patch + j, 4)]
            total += jnp.dot(weights[:, (j - 1) * PATCH : j * PATCH], values, preferred_element_type=F32)
        o_stale[rows, :] = total

    wait_weights(1)
    project(1, k_v)

    @pl.loop(0, PATCH // Q_STEP)
    def _(i):
        rows = pl.ds(pl.multiple_of(i * Q_STEP, Q_STEP), Q_STEP)
        scores = lax.dot_general(q_v[rows, :], k_v[...], NT, preferred_element_type=F32) * scaling
        top = jnp.max(scores, axis=1, keepdims=True)
        expo = jnp.exp(scores - top)
        l_part = jnp.broadcast_to(jnp.sum(expo, axis=1, keepdims=True), (Q_STEP, HD))
        top = jnp.broadcast_to(top, (Q_STEP, HD))
        high = jnp.maximum(top, m_stale[rows, :])
        a_new = jnp.exp(top - high)
        a_old = jnp.exp(m_stale[rows, :] - high)
        inverse = 1.0 / (a_new * l_part + a_old * l_stale[rows, :])
        m_new[rows, :] = a_new * inverse
        o_stale[rows, :] = o_stale[rows, :] * (a_old * inverse)
        p_new[rows, :] = expo.astype(BF16)

    wait_weights(2)
    project(2, v_v)

    @pl.loop(0, PATCH // Q_STEP)
    def _(i):
        rows = pl.ds(pl.multiple_of(i * Q_STEP, Q_STEP), Q_STEP)
        fresh = jnp.dot(p_new[rows, :], v_v[...], preferred_element_type=F32)
        attg[x, rows, :] = (o_stale[rows, :] + fresh * m_new[rows, :]).astype(BF16)

    def send_a(slot, e, sem):
        return pltpu.make_async_remote_copy(
            attg.at[slot], attg.at[slot], sem, rs_a.at[slot],
            device_id=(section, lax.rem(x + e, 4) * 4 + zh), device_id_type=MESH,
        )

    for e in range(1, 4):
        send_a(x, e, ss_a.at[e - 1]).start()
    for e in range(1, 4):
        send_a(lax.rem(x + e, 4), e, ss_a.at[e - 1]).wait_recv()

    def along(sign):
        return (section, x * 4 + lax.rem(zh + 4 + sign, 4))

    def remote(src, dst, k, c, sign):
        return pltpu.make_async_remote_copy(
            src, dst, ss_r.at[k, c], rs_r.at[k, c], device_id=along(sign), device_id_type=MESH
        )

    low, high = pl.ds(0, HALF), pl.ds(HALF, HALF)

    def far_up(c):
        return remote(part.at[0, c, low], far_in.at[0, c], 0, c, 1)

    def far_down(c):
        return remote(part.at[0, c, high], far_in.at[1, c], 1, c, -1)

    def plain_up(c):
        return remote(part.at[1, c, high], near_in.at[0, c, high], 2, c, 1)

    def plain_down(c):
        return remote(part.at[2, c, low], near_in.at[1, c, low], 3, c, -1)

    def sum_up(c):
        return remote(part.at[1, c, low], near_in.at[0, c, low], 4, c, 1)

    def sum_down(c):
        return remote(part.at[2, c, high], near_in.at[1, c, high], 5, c, -1)

    at = lax.rem(y, 4)
    rising = 228 - 3 * at - 84 * at * (at - 1) + 52 * at * (at - 1) * (at - 2)
    falling = 27 + 48 * at + 33 * ((at * (at - 1)) // 2) - 7 * at * (at - 1) * (at - 2)
    other = lax.rem(y // 4 + lax.rem(x, 2), 2)

    def quarter(i, code):
        group = lax.rem(code, 4)
        step = lax.rem(group - zh + 4, 4)
        features = pl.ds(pl.multiple_of(group * SHARE, SHARE), SHARE)
        view = wqkv.at[0, pl.ds(0, 8 * ROWS)]
        pltpu.make_async_copy(view, view, rs_o.at[group]).wait()
        weights = jnp.concatenate([wo[j, features, :] for j in range(4)], axis=1)

        @pl.loop(0, CHUNKS)
        def _(c):
            tokens = pl.ds(pl.multiple_of(c * HD, HD), HD)
            attended = jnp.concatenate([attg[j, tokens, :] for j in range(4)], axis=1)
            quarters[step, c] = lax.dot_general(weights, attended, NT, preferred_element_type=F32)

            @pl.when(step == 2)
            def _():
                part[0, c] = quarters[2, c].astype(BF16)
                far_up(c).start()
                far_down(c).start()

            @pl.when(step == 1)
            def _():
                part[1, c, high, :] = quarters[1, c, high, :].astype(BF16)
                plain_up(c).start()

            @pl.when(step == 3)
            def _():
                part[2, c, low, :] = quarters[3, c, low, :].astype(BF16)
                plain_down(c).start()

        return code // 4

    lax.fori_loop(0, 4, quarter, other * rising + (1 - other) * falling)

    @pl.loop(0, CHUNKS)
    def _(c):
        far_up(c).wait_recv()
        part[1, c, low, :] = (quarters[1, c, low, :] + far_in[0, c].astype(F32)).astype(BF16)
        sum_up(c).start()
        far_down(c).wait_recv()
        part[2, c, high, :] = (quarters[3, c, high, :] + far_in[1, c].astype(F32)).astype(BF16)
        sum_down(c).start()

    def hand(c):
        tokens = pl.ds(pl.multiple_of(c * HD, HD), HD)
        return pltpu.make_async_remote_copy(
            res.at[c], out_ref.at[:, tokens], ss_h.at[c], rs_h.at[c],
            device_id=(lax.rem(section + 1, BLOCKS), t), device_id_type=MESH,
        )

    @pl.loop(0, CHUNKS)
    def _(c):
        for copy in (plain_up, plain_down, sum_up, sum_down):
            copy(c).wait_recv()
        tokens = pl.ds(pl.multiple_of(c * HD, HD), HD)
        mixed = quarters[0, c] + near_in[0, c].astype(F32) + near_in[1, c].astype(F32)
        gate = columns[2, my_features, :]
        res[c] = (xg[my_features, tokens].astype(F32) + gate * mixed).astype(BF16)
        hand(c).start()

    for p in range(4):
        view = wqkv.at[0, pl.ds(0, D - ROWS)]
        pltpu.make_async_copy(view, view, ss_w.at[p]).wait()

    @pl.when(xo != x)
    def _():
        send_o(BLOCKS - 1, ss_own).wait_send()

    for d in range(6):
        send_x(t, (section, t), ss_x.at[d]).wait_send()
    for d in range(9):
        send_x(t, (section, t), ss_f.at[d]).wait_send()
    for d in range(3):
        send_a(x, d + 1, ss_a.at[d]).wait_send()

    @pl.loop(0, CHUNKS)
    def _(c):
        for copy in (far_up, far_down, plain_up, plain_down, sum_up, sum_down):
            copy(c).wait_send()
        hand(c).wait()


def local(block_weights, modulation, inflow, stale_cache, patch_index, assignment):
    vmem = pl.BlockSpec(memory_space=pltpu.VMEM)
    smem = pl.BlockSpec(memory_space=pltpu.SMEM)
    hbm = pl.BlockSpec(memory_space=pltpu.HBM)
    dma = pltpu.SemaphoreType.DMA
    result = pl.pallas_call(
        kernel,
        out_shape=jax.ShapeDtypeStruct((SHARE, PATCH), BF16),
        in_specs=[smem, smem, hbm, hbm, hbm, hbm],
        out_specs=vmem,
        scratch_shapes=[
            pltpu.VMEM((BLOCKS, 4 * ROWS, HD), BF16),
            pltpu.VMEM((3, 1, D), F32),
            pltpu.VMEM((3, D, HD), F32),
            pltpu.VMEM((2, 4, PATCH, HD), BF16),
            pltpu.VMEM((4 * ROWS, 4 * ROWS), BF16),
            pltpu.VMEM((BLOCKS, 4 * ROWS, HD), BF16),
            pltpu.VMEM((3, D, HD), BF16),
            pltpu.VMEM((4, PER_X, HD), BF16),
            pltpu.VMEM((D, PATCH), BF16),
            pltpu.VMEM((PATCH, D), BF16),
            pltpu.VMEM((PATCH, HD), BF16),
            pltpu.VMEM((PATCH, HD), BF16),
            pltpu.VMEM((PATCH, HD), BF16),
            pltpu.VMEM((PATCH, HD), F32),
            pltpu.VMEM((PATCH, HD), F32),
            pltpu.VMEM((PATCH, HD), F32),
            pltpu.VMEM((PATCH, PATCH), BF16),
            pltpu.VMEM((PATCH, HD), F32),
            pltpu.VMEM((4, PATCH, HD), BF16),
            pltpu.VMEM((N_TP, 2, PATCH), F32),
            pltpu.VMEM((8, PATCH), F32),
            pltpu.VMEM((4, CHUNKS, SHARE, HD), F32),
            pltpu.VMEM((3, CHUNKS, SHARE, HD), BF16),
            pltpu.VMEM((2, CHUNKS, HALF, HD), BF16),
            pltpu.VMEM((2, CHUNKS, SHARE, HD), BF16),
            pltpu.VMEM((CHUNKS, SHARE, HD), BF16),
            dma((4,)), dma((4,)), dma((3,)), dma((4,)), dma,
            dma((6,)), dma((N_TP,)), dma((9,)), dma((3,)), dma((4,)), dma((6, CHUNKS)), dma((6, CHUNKS)), dma((CHUNKS,)), dma((CHUNKS,)),
        ],
        compiler_params=pltpu.CompilerParams(
            collective_id=0, has_side_effects=True, vmem_limit_bytes=60 * 2**20
        ),
    )(
        assignment,
        patch_index,
        block_weights.reshape(BLOCKS, 4 * ROWS, HD),
        modulation.transpose(1, 0, 2),
        inflow[0].T,
        stale_cache.reshape(2, 4, PATCH, HD),
    )
    return result.T[None]


def solution(mesh):
    placed = (
        P(None, "section", None, "tp"),
        P("section", None, None),
        P("section", None, "tp"),
        P("section", None, None, "tp"),
        P("section"),
        P(),
    )
    return jax.shard_map(
        local, mesh=mesh, in_specs=placed, out_specs=P("section", None, "tp"), check_vma=False
    )
```

```python
import functools

import jax
import jax.numpy as jnp
from jax import lax
from jax.experimental import pallas as pl
from jax.experimental.pallas import tpu as pltpu
from jax.sharding import PartitionSpec as P

MESH = pl.DeviceIdType.MESH
F32 = jnp.float32
BF16 = jnp.bfloat16

HD = 128
D = 3072
PATCH = 512
SEQ = 2048
BLOCKS = 32
N_TP = 16
ROWS = D // BLOCKS
SHARE = D // N_TP
HALF = SHARE // 2
CHUNKS = PATCH // HD
PER_X = D // 4
Q_STEP = 128


def peer_section(k, section):
    core = lax.rem(section, 2)
    y = lax.rem(section // 2, 8)
    z_lo = section // 16
    turn = k // 4
    flip = 3 - lax.rem(k, 4)
    half = (turn + 1) // 2
    dy = 4 + half * (1 - 2 * lax.rem(turn, 2))
    return (lax.rem(z_lo + flip // 2, 2) * 8 + lax.rem(y + dy, 8)) * 2 + lax.rem(core + lax.rem(flip, 2), 2)


def kernel(
    assign_ref, patch_ref, w_hbm, mod_hbm, x_hbm, stale_hbm, out_ref,
    w_v, mod_v, columns, stale_v, perm_v, send_w, wqkv, wo, xg, normed, q_v, k_v, v_v,
    o_stale, m_stale, l_stale, p_new, m_new, attg, stats, norm_v, quarters, part, far_in, near_in, res,
    sem_loc, ss_w, rs_w, rs_o, ss_own, ss_x, rs_x, ss_f, ss_a, rs_a, ss_r, rs_r, ss_h, rs_h,
):
    section = lax.axis_index("section")
    t = lax.axis_index("tp")
    x = t // 4
    zh = lax.rem(t, 4)
    y = lax.rem(section // 2, 8)
    xo = section // 8

    load_w = pltpu.make_async_copy(w_hbm, w_v, sem_loc.at[0])
    my_features = pl.ds(pl.multiple_of(t * SHARE, SHARE), SHARE)
    load_x = pltpu.make_async_copy(x_hbm, xg.at[my_features], sem_loc.at[1])
    load_s = pltpu.make_async_copy(stale_hbm, stale_v, sem_loc.at[2])
    load_m = pltpu.make_async_copy(mod_hbm, mod_v, sem_loc.at[3])
    load_x.start()
    load_w.start()
    load_m.start()
    load_s.start()

    barrier = pltpu.get_barrier_semaphore()

    def greet(dev):
        pl.semaphore_signal(barrier, inc=1, device_id=dev, device_id_type=MESH)

    @pl.loop(0, BLOCKS - 1)
    def _(k):
        greet((peer_section(k, section), t))

    @pl.loop(0, BLOCKS)
    def _(k):
        greet((x * 8 + k // 4, lax.rem(k, 4) * 4 + zh))

    for d in range(1, 4):
        greet((section, lax.rem(x + d, 4) * 4 + zh))
        greet((section, x * 4 + lax.rem(zh + d, 4)))

    row = lax.broadcasted_iota(jnp.int32, (4 * ROWS, 4 * ROWS), 0)
    col = lax.broadcasted_iota(jnp.int32, (4 * ROWS, 4 * ROWS), 1)
    proj = (row >= ROWS).astype(jnp.int32) + (row >= 2 * ROWS).astype(jnp.int32) + (row >= 3 * ROWS).astype(jnp.int32)
    perm_v[...] = jnp.where(col == (row - proj * ROWS) * 4 + proj, 1.0, 0.0).astype(BF16)

    load_x.wait()
    load_w.wait()

    pl.semaphore_wait(barrier, (BLOCKS - 1) + BLOCKS + 6)

    def send_x(slot, dev, sem):
        rows = pl.ds(pl.multiple_of(slot * SHARE, SHARE), SHARE)
        return pltpu.make_async_remote_copy(
            xg.at[rows], xg.at[rows], sem, rs_x.at[slot], device_id=dev, device_id_type=MESH
        )

    def send_z(d):
        return send_x(t, (section, x * 4 + lax.rem(zh + d, 4)), ss_x.at[d - 1])

    def pass_on(d):
        slot = x * 4 + lax.rem(zh + d, 4)
        send_x(slot, (section, slot), ss_x.at[0]).wait_recv()
        for e in range(1, 4):
            dev = (section, lax.rem(x + e, 4) * 4 + zh)
            send_x(slot, dev, ss_f.at[3 * (d - 1) + e - 1]).start()

    send_z(1).start()
    send_z(3).start()
    send_z(2).start()
    for d in range(1, 4):
        send_x(t, (section, lax.rem(x + d, 4) * 4 + zh), ss_x.at[2 + d]).start()

    def block_of(s):
        owner = jnp.int32(0)
        for b in range(1, BLOCKS):
            owner = jnp.where(assign_ref[b] == s, b, owner)
        return w_v[owner]

    my_rows = pl.ds(pl.multiple_of(section * ROWS, ROWS), ROWS)

    def send_part(k, p):
        return pltpu.make_async_remote_copy(
            send_w.at[k, pl.ds(p * ROWS, ROWS)], wqkv.at[p, my_rows], ss_w.at[p], rs_w.at[p],
            device_id=(peer_section(k, section), t), device_id_type=MESH,
        )

    o_rows = pl.ds(pl.multiple_of(lax.rem(section, 8) * ROWS, ROWS), ROWS)
    o_group = lax.rem(section // 2, 4)

    def send_o(k, sem):
        return pltpu.make_async_remote_copy(
            send_w.at[k, pl.ds(3 * ROWS, ROWS)], wo.at[x, o_rows], sem, rs_o.at[o_group],
            device_id=(peer_section(k, section), xo * 4 + zh), device_id_type=MESH,
        )

    @pl.loop(0, BLOCKS // 4)
    def _(g):
        blocks = jnp.concatenate([block_of(peer_section(4 * g + i, section)) for i in range(4)], axis=1)
        ordered = jnp.dot(perm_v[...], blocks, preferred_element_type=F32).astype(BF16)
        for i in range(4):
            send_w[4 * g + i] = ordered[:, i * HD : (i + 1) * HD]
        for i in range(3):
            send_part(4 * g + i, 0).start()

        @pl.when(g < BLOCKS // 4 - 1)
        def _():
            send_part(4 * g + 3, 0).start()

    for p in range(3):
        wqkv[p, my_rows, :] = send_w[BLOCKS - 1, pl.ds(p * ROWS, ROWS), :]
    pass_on(1)
    pass_on(3)

    @pl.loop(0, BLOCKS - 1)
    def _(k):
        send_part(k, 1).start()

    pass_on(2)

    @pl.loop(0, BLOCKS - 1)
    def _(k):
        send_part(k, 2).start()

    @pl.loop(0, BLOCKS - 1)
    def _(k):
        send_o(k, ss_w.at[3]).start()

    own_o = pltpu.make_async_copy(
        send_w.at[BLOCKS - 1, pl.ds(3 * ROWS, ROWS)], wo.at[x, o_rows], rs_o.at[o_group]
    )

    @pl.when(xo == x)
    def _():
        own_o.start()

    @pl.when(xo != x)
    def _():
        send_o(BLOCKS - 1, ss_own).start()

    load_m.wait()

    @pl.loop(0, D // HD)
    def _(c):
        features = pl.ds(pl.multiple_of(c * HD, HD), HD)
        for p in range(3):
            columns[p, features, :] = jnp.broadcast_to(mod_v[p, :, features], (HD, HD)).T

    def take_stats(slot):
        rows = pl.ds(pl.multiple_of(slot * SHARE, SHARE), SHARE)
        tokens = xg[rows, :].astype(F32)
        mean = jnp.sum(jnp.sum(tokens.reshape(SHARE // 8, 8, PATCH), axis=0), axis=0, keepdims=True) / SHARE
        shifted = tokens - mean
        shifted = shifted * shifted
        moment = jnp.sum(jnp.sum(shifted.reshape(SHARE // 8, 8, PATCH), axis=0), axis=0, keepdims=True)
        stats[slot] = jnp.concatenate([mean, moment], axis=0)

    @pl.loop(0, 4)
    def _(d):
        take_stats(x * 4 + lax.rem(zh + d, 4))

    @pl.loop(0, 12)
    def _(i):
        slot = lax.rem(x + 1 + lax.rem(i, 3), 4) * 4 + lax.rem(zh + i // 3, 4)
        send_x(slot, (section, slot), ss_x.at[0]).wait_recv()
        take_stats(slot)

    means = stats[:, 0, :]
    center = jnp.sum(means, axis=0, keepdims=True) / N_TP
    means = means - center
    moment = jnp.sum(stats[:, 1, :] + SHARE * means * means, axis=0, keepdims=True)
    inverse = lax.rsqrt(moment / D + 1e-06)
    norm_v[0:1, :] = center
    norm_v[1:2, :] = inverse

    @pl.loop(0, D // HD)
    def _(c):
        features = pl.ds(pl.multiple_of(c * HD, HD), HD)
        scale = 1.0 + columns[0, features, :]
        shift = columns[1, features, :]
        for i in range(PATCH // HD):
            tokens = pl.ds(i * HD, HD)
            value = (xg[features, tokens].astype(F32) - norm_v[0:1, tokens]) * norm_v[1:2, tokens]
            normed[tokens, features] = (value * scale + shift).T.astype(BF16)

    def wait_weights(p):
        view = wqkv.at[p, pl.ds(0, D - ROWS)]
        pltpu.make_async_copy(view, view, rs_w.at[p]).wait()

    def project(p, dst):
        @pl.loop(0, PATCH // Q_STEP)
        def _(i):
            rows = pl.ds(pl.multiple_of(i * Q_STEP, Q_STEP), Q_STEP)
            dst[rows, :] = jnp.dot(normed[rows, :], wqkv[p], preferred_element_type=F32).astype(BF16)

    NT = (((1,), (1,)), ((), ()))
    scaling = HD ** -0.5

    wait_weights(0)
    project(0, q_v)
    load_s.wait()
    patch = patch_ref[0]

    @pl.loop(0, PATCH // Q_STEP)
    def _(i):
        rows = pl.ds(pl.multiple_of(i * Q_STEP, Q_STEP), Q_STEP)
        query = q_v[rows, :]
        scores = []
        for j in range(1, 4):
            keys = stale_v[0, lax.rem(patch + j, 4)]
            scores.append(lax.dot_general(query, keys, NT, preferred_element_type=F32) * scaling)
        scores = jnp.concatenate(scores, axis=1)
        top = jnp.max(scores, axis=1, keepdims=True)
        expo = jnp.exp(scores - top)
        m_stale[rows, :] = jnp.broadcast_to(top, (Q_STEP, HD))
        l_stale[rows, :] = jnp.broadcast_to(jnp.sum(expo, axis=1, keepdims=True), (Q_STEP, HD))
        weights = expo.astype(BF16)
        total = jnp.zeros((Q_STEP, HD), F32)
        for j in range(1, 4):
            values = stale_v[1, lax.rem(patch + j, 4)]
            total += jnp.dot(weights[:, (j - 1) * PATCH : j * PATCH], values, preferred_element_type=F32)
        o_stale[rows, :] = total

    wait_weights(1)
    project(1, k_v)

    @pl.loop(0, PATCH // Q_STEP)
    def _(i):
        rows = pl.ds(pl.multiple_of(i * Q_STEP, Q_STEP), Q_STEP)
        scores = lax.dot_general(q_v[rows, :], k_v[...], NT, preferred_element_type=F32) * scaling
        top = jnp.max(scores, axis=1, keepdims=True)
        expo = jnp.exp(scores - top)
        l_part = jnp.broadcast_to(jnp.sum(expo, axis=1, keepdims=True), (Q_STEP, HD))
        top = jnp.broadcast_to(top, (Q_STEP, HD))
        high = jnp.maximum(top, m_stale[rows, :])
        a_new = jnp.exp(top - high)
        a_old = jnp.exp(m_stale[rows, :] - high)
        inverse = 1.0 / (a_new * l_part + a_old * l_stale[rows, :])
        m_new[rows, :] = a_new * inverse
        o_stale[rows, :] = o_stale[rows, :] * (a_old * inverse)
        p_new[rows, :] = expo.astype(BF16)

    def send_a(slot, c, e):
        rows = pl.ds(pl.multiple_of(c * Q_STEP, Q_STEP), Q_STEP)
        return pltpu.make_async_remote_copy(
            attg.at[slot, rows], attg.at[slot, rows], ss_a.at[e - 1, c], rs_a.at[slot, c],
            device_id=(section, lax.rem(x + e, 4) * 4 + zh), device_id_type=MESH,
        )

    wait_weights(2)
    project(2, v_v)

    @pl.loop(0, CHUNKS)
    def _(c):
        rows = pl.ds(pl.multiple_of(c * Q_STEP, Q_STEP), Q_STEP)
        fresh = jnp.dot(p_new[rows, :], v_v[...], preferred_element_type=F32)
        attg[x, rows, :] = (o_stale[rows, :] + fresh * m_new[rows, :]).astype(BF16)
        for e in range(1, 4):
            send_a(x, c, e).start()

    def along(sign):
        return (section, x * 4 + lax.rem(zh + 4 + sign, 4))

    def remote(src, dst, k, c, sign):
        return pltpu.make_async_remote_copy(
            src, dst, ss_r.at[k, c], rs_r.at[k, c], device_id=along(sign), device_id_type=MESH
        )

    low, high = pl.ds(0, HALF), pl.ds(HALF, HALF)

    def far_up(c):
        return remote(part.at[0, c, low], far_in.at[0, c], 0, c, 1)

    def far_down(c):
        return remote(part.at[0, c, high], far_in.at[1, c], 1, c, -1)

    def plain_up(c):
        return remote(part.at[1, c, high], near_in.at[0, c, high], 2, c, 1)

    def plain_down(c):
        return remote(part.at[2, c, low], near_in.at[1, c, low], 3, c, -1)

    def sum_up(c):
        return remote(part.at[1, c, low], near_in.at[0, c, low], 4, c, 1)

    def sum_down(c):
        return remote(part.at[2, c, high], near_in.at[1, c, high], 5, c, -1)

    for step in (2, 1, 3, 0):
        group = lax.rem(zh + step, 4)
        features = pl.ds(pl.multiple_of(group * SHARE, SHARE), SHARE)
        view = wqkv.at[0, pl.ds(0, 8 * ROWS)]
        pltpu.make_async_copy(view, view, rs_o.at[group]).wait()
        weights = jnp.concatenate([wo[j, features, :] for j in range(4)], axis=1)

        @pl.loop(0, CHUNKS)
        def _(c):
            tokens = pl.ds(pl.multiple_of(c * HD, HD), HD)
            if step == 2:
                for e in range(1, 4):
                    send_a(lax.rem(x + e, 4), c, e).wait_recv()
            attended = jnp.concatenate([attg[j, tokens, :] for j in range(4)], axis=1)
            value = lax.dot_general(weights, attended, NT, preferred_element_type=F32)
            if step == 2:
                part[0, c] = value.astype(BF16)
                far_up(c).start()
                far_down(c).start()
            elif step == 1:
                quarters[1, c] = value
                part[1, c, high, :] = value[HALF:].astype(BF16)
                plain_up(c).start()
            elif step == 3:
                quarters[2, c] = value
                part[2, c, low, :] = value[:HALF].astype(BF16)
                plain_down(c).start()
            else:
                quarters[0, c] = value

    @pl.loop(0, CHUNKS)
    def _(c):
        far_up(c).wait_recv()
        part[1, c, low, :] = (quarters[1, c, low, :] + far_in[0, c].astype(F32)).astype(BF16)
        sum_up(c).start()
        far_down(c).wait_recv()
        part[2, c, high, :] = (quarters[2, c, high, :] + far_in[1, c].astype(F32)).astype(BF16)
        sum_down(c).start()

    def hand(c):
        tokens = pl.ds(pl.multiple_of(c * HD, HD), HD)
        return pltpu.make_async_remote_copy(
            res.at[c], out_ref.at[:, tokens], ss_h.at[c], rs_h.at[c],
            device_id=(lax.rem(section + 1, BLOCKS), t), device_id_type=MESH,
        )

    @pl.loop(0, CHUNKS)
    def _(c):
        for copy in (plain_up, plain_down, sum_up, sum_down):
            copy(c).wait_recv()
        tokens = pl.ds(pl.multiple_of(c * HD, HD), HD)
        mixed = quarters[0, c] + near_in[0, c].astype(F32) + near_in[1, c].astype(F32)
        gate = columns[2, my_features, :]
        res[c] = (xg[my_features, tokens].astype(F32) + gate * mixed).astype(BF16)
        hand(c).start()

    for p in range(4):
        view = wqkv.at[0, pl.ds(0, D - ROWS)]
        pltpu.make_async_copy(view, view, ss_w.at[p]).wait()

    @pl.when(xo != x)
    def _():
        send_o(BLOCKS - 1, ss_own).wait_send()

    for d in range(6):
        send_x(t, (section, t), ss_x.at[d]).wait_send()
    for d in range(9):
        send_x(t, (section, t), ss_f.at[d]).wait_send()

    @pl.loop(0, CHUNKS)
    def _(c):
        for copy in (far_up, far_down, plain_up, plain_down, sum_up, sum_down):
            copy(c).wait_send()
        for e in range(1, 4):
            send_a(x, c, e).wait_send()
        hand(c).wait()


def local(block_weights, modulation, inflow, stale_cache, patch_index, assignment):
    smem = pl.BlockSpec(memory_space=pltpu.SMEM)
    hbm = pl.BlockSpec(memory_space=pltpu.HBM)
    dma = pltpu.SemaphoreType.DMA
    result = pl.pallas_call(
        kernel,
        out_shape=jax.ShapeDtypeStruct((SHARE, PATCH), BF16),
        in_specs=[smem, smem, hbm, hbm, hbm, hbm],
        out_specs=hbm,
        scratch_shapes=[
            pltpu.VMEM((BLOCKS, 4 * ROWS, HD), BF16),
            pltpu.VMEM((3, 1, D), F32),
            pltpu.VMEM((3, D, HD), F32),
            pltpu.VMEM((2, 4, PATCH, HD), BF16),
            pltpu.VMEM((4 * ROWS, 4 * ROWS), BF16),
            pltpu.VMEM((BLOCKS, 4 * ROWS, HD), BF16),
            pltpu.VMEM((3, D, HD), BF16),
            pltpu.VMEM((4, PER_X, HD), BF16),
            pltpu.VMEM((D, PATCH), BF16),
            pltpu.VMEM((PATCH, D), BF16),
            pltpu.VMEM((PATCH, HD), BF16),
            pltpu.VMEM((PATCH, HD), BF16),
            pltpu.VMEM((PATCH, HD), BF16),
            pltpu.VMEM((PATCH, HD), F32),
            pltpu.VMEM((PATCH, HD), F32),
            pltpu.VMEM((PATCH, HD), F32),
            pltpu.VMEM((PATCH, PATCH), BF16),
            pltpu.VMEM((PATCH, HD), F32),
            pltpu.VMEM((4, PATCH, HD), BF16),
            pltpu.VMEM((N_TP, 2, PATCH), F32),
            pltpu.VMEM((8, PATCH), F32),
            pltpu.VMEM((3, CHUNKS, SHARE, HD), F32),
            pltpu.VMEM((3, CHUNKS, SHARE, HD), BF16),
            pltpu.VMEM((2, CHUNKS, HALF, HD), BF16),
            pltpu.VMEM((2, CHUNKS, SHARE, HD), BF16),
            pltpu.VMEM((CHUNKS, SHARE, HD), BF16),
            dma((4,)), dma((4,)), dma((3,)), dma((4,)), dma,
            dma((6,)), dma((N_TP,)), dma((9,)), dma((3, CHUNKS)), dma((4, CHUNKS)), dma((6, CHUNKS)), dma((6, CHUNKS)), dma((CHUNKS,)), dma((CHUNKS,)),
        ],
        compiler_params=pltpu.CompilerParams(
            collective_id=0, has_side_effects=True, vmem_limit_bytes=60 * 2**20
        ),
    )(
        assignment,
        patch_index,
        block_weights.reshape(BLOCKS, 4 * ROWS, HD),
        modulation.transpose(1, 0, 2),
        inflow[0].T,
        stale_cache.reshape(2, 4, PATCH, HD),
    )
    return result.T[None]


def solution(mesh):
    placed = (
        P(None, "section", None, "tp"),
        P("section", None, None),
        P("section", None, "tp"),
        P("section", None, None, "tp"),
        P("section"),
        P(),
    )
    return jax.shard_map(
        local, mesh=mesh, in_specs=placed, out_specs=P("section", None, "tp"), check_vma=False
    )
```

```python
import functools

import jax
import jax.numpy as jnp
from jax import lax
from jax.experimental import pallas as pl
from jax.experimental.pallas import tpu as pltpu
from jax.sharding import PartitionSpec as P

MESH = pl.DeviceIdType.MESH
F32 = jnp.float32
BF16 = jnp.bfloat16

HD = 128
D = 3072
PATCH = 512
SEQ = 2048
BLOCKS = 32
N_TP = 16
ROWS = D // BLOCKS
SHARE = D // N_TP
HALF = SHARE // 2
CHUNKS = PATCH // HD
PER_X = D // 4
Q_STEP = 128


def peer_section(k, section):
    core = lax.rem(section, 2)
    y = lax.rem(section // 2, 8)
    z_lo = section // 16
    turn = k // 4
    flip = 3 - lax.rem(k, 4)
    half = (turn + 1) // 2
    dy = 4 + half * (1 - 2 * lax.rem(turn, 2))
    return (lax.rem(z_lo + flip // 2, 2) * 8 + lax.rem(y + dy, 8)) * 2 + lax.rem(core + lax.rem(flip, 2), 2)


def kernel(
    assign_ref, patch_ref, w_hbm, mod_hbm, x_hbm, stale_hbm, out_ref,
    w_v, mod_v, columns, stale_v, perm_v, send_w, wqkv, wo, xg, normed, q_v, k_v, v_v,
    o_stale, m_stale, l_stale, p_new, m_new, attg, stats, norm_v, quarters, part, far_in, near_in, res,
    sem_loc, ss_w, rs_w, rs_o, ss_own, ss_x, rs_x, ss_f, ss_a, rs_a, ss_r, rs_r, ss_h, rs_h,
):
    section = lax.axis_index("section")
    t = lax.axis_index("tp")
    x = t // 4
    zh = lax.rem(t, 4)
    y = lax.rem(section // 2, 8)
    xo = section // 8

    load_w = pltpu.make_async_copy(w_hbm, w_v, sem_loc.at[0])
    my_features = pl.ds(pl.multiple_of(t * SHARE, SHARE), SHARE)
    load_x = pltpu.make_async_copy(x_hbm, xg.at[my_features], sem_loc.at[1])
    load_s = pltpu.make_async_copy(stale_hbm, stale_v, sem_loc.at[2])
    load_m = pltpu.make_async_copy(mod_hbm, mod_v, sem_loc.at[3])
    load_x.start()
    load_w.start()
    load_m.start()
    load_s.start()

    barrier = pltpu.get_barrier_semaphore()

    def greet(dev):
        pl.semaphore_signal(barrier, inc=1, device_id=dev, device_id_type=MESH)

    @pl.loop(0, BLOCKS - 1)
    def _(k):
        greet((peer_section(k, section), t))

    @pl.loop(0, BLOCKS)
    def _(k):
        greet((x * 8 + k // 4, lax.rem(k, 4) * 4 + zh))

    for d in range(1, 4):
        greet((section, lax.rem(x + d, 4) * 4 + zh))
        greet((section, x * 4 + lax.rem(zh + d, 4)))

    row = lax.broadcasted_iota(jnp.int32, (4 * ROWS, 4 * ROWS), 0)
    col = lax.broadcasted_iota(jnp.int32, (4 * ROWS, 4 * ROWS), 1)
    proj = (row >= ROWS).astype(jnp.int32) + (row >= 2 * ROWS).astype(jnp.int32) + (row >= 3 * ROWS).astype(jnp.int32)
    perm_v[...] = jnp.where(col == (row - proj * ROWS) * 4 + proj, 1.0, 0.0).astype(BF16)

    load_x.wait()
    load_w.wait()

    pl.semaphore_wait(barrier, (BLOCKS - 1) + BLOCKS + 6)

    def send_x(slot, dev, sem):
        rows = pl.ds(pl.multiple_of(slot * SHARE, SHARE), SHARE)
        return pltpu.make_async_remote_copy(
            xg.at[rows], xg.at[rows], sem, rs_x.at[slot], device_id=dev, device_id_type=MESH
        )

    def send_z(d):
        return send_x(t, (section, x * 4 + lax.rem(zh + d, 4)), ss_x.at[d - 1])

    def pass_on(d):
        slot = x * 4 + lax.rem(zh + d, 4)
        send_x(slot, (section, slot), ss_x.at[0]).wait_recv()
        for e in range(1, 4):
            dev = (section, lax.rem(x + e, 4) * 4 + zh)
            send_x(slot, dev, ss_f.at[3 * (d - 1) + e - 1]).start()

    send_z(1).start()
    send_z(3).start()
    send_z(2).start()
    for d in range(1, 4):
        send_x(t, (section, lax.rem(x + d, 4) * 4 + zh), ss_x.at[2 + d]).start()

    def block_of(s):
        owner = jnp.int32(0)
        for b in range(1, BLOCKS):
            owner = jnp.where(assign_ref[b] == s, b, owner)
        return w_v[owner]

    my_rows = pl.ds(pl.multiple_of(section * ROWS, ROWS), ROWS)

    def send_part(k, p):
        return pltpu.make_async_remote_copy(
            send_w.at[k, pl.ds(p * ROWS, ROWS)], wqkv.at[p, my_rows], ss_w.at[p], rs_w.at[p],
            device_id=(peer_section(k, section), t), device_id_type=MESH,
        )

    o_rows = pl.ds(pl.multiple_of(lax.rem(section, 8) * ROWS, ROWS), ROWS)
    o_group = lax.rem(section // 2, 4)

    def send_o(k, sem):
        return pltpu.make_async_remote_copy(
            send_w.at[k, pl.ds(3 * ROWS, ROWS)], wo.at[x, o_rows], sem, rs_o.at[o_group],
            device_id=(peer_section(k, section), xo * 4 + zh), device_id_type=MESH,
        )

    @pl.loop(0, BLOCKS // 4)
    def _(g):
        blocks = jnp.concatenate([block_of(peer_section(4 * g + i, section)) for i in range(4)], axis=1)
        ordered = jnp.dot(perm_v[...], blocks, preferred_element_type=F32).astype(BF16)
        for i in range(4):
            send_w[4 * g + i] = ordered[:, i * HD : (i + 1) * HD]
        for i in range(3):
            send_part(4 * g + i, 0).start()

        @pl.when(g < BLOCKS // 4 - 1)
        def _():
            send_part(4 * g + 3, 0).start()

    for p in range(3):
        wqkv[p, my_rows, :] = send_w[BLOCKS - 1, pl.ds(p * ROWS, ROWS), :]
    @pl.loop(0, BLOCKS - 1)
    def _(k):
        send_part(k, 1).start()

    pass_on(1)
    pass_on(3)

    @pl.loop(0, BLOCKS - 1)
    def _(k):
        send_part(k, 2).start()

    pass_on(2)

    @pl.loop(0, BLOCKS - 1)
    def _(k):
        send_o(k, ss_w.at[3]).start()

    own_o = pltpu.make_async_copy(
        send_w.at[BLOCKS - 1, pl.ds(3 * ROWS, ROWS)], wo.at[x, o_rows], rs_o.at[o_group]
    )

    @pl.when(xo == x)
    def _():
        own_o.start()

    @pl.when(xo != x)
    def _():
        send_o(BLOCKS - 1, ss_own).start()

    load_m.wait()

    @pl.loop(0, D // HD)
    def _(c):
        features = pl.ds(pl.multiple_of(c * HD, HD), HD)
        for p in range(3):
            columns[p, features, :] = jnp.broadcast_to(mod_v[p, :, features], (HD, HD)).T

    def take_stats(slot):
        rows = pl.ds(pl.multiple_of(slot * SHARE, SHARE), SHARE)
        tokens = xg[rows, :].astype(F32)
        mean = jnp.sum(jnp.sum(tokens.reshape(SHARE // 8, 8, PATCH), axis=0), axis=0, keepdims=True) / SHARE
        shifted = tokens - mean
        shifted = shifted * shifted
        moment = jnp.sum(jnp.sum(shifted.reshape(SHARE // 8, 8, PATCH), axis=0), axis=0, keepdims=True)
        stats[slot] = jnp.concatenate([mean, moment], axis=0)

    @pl.loop(0, 4)
    def _(d):
        take_stats(x * 4 + lax.rem(zh + d, 4))

    @pl.loop(0, 12)
    def _(i):
        slot = lax.rem(x + 1 + lax.rem(i, 3), 4) * 4 + lax.rem(zh + i // 3, 4)
        send_x(slot, (section, slot), ss_x.at[0]).wait_recv()
        take_stats(slot)

    means = stats[:, 0, :]
    center = jnp.sum(means, axis=0, keepdims=True) / N_TP
    means = means - center
    moment = jnp.sum(stats[:, 1, :] + SHARE * means * means, axis=0, keepdims=True)
    inverse = lax.rsqrt(moment / D + 1e-06)
    norm_v[0:1, :] = center
    norm_v[1:2, :] = inverse

    @pl.loop(0, D // HD)
    def _(c):
        features = pl.ds(pl.multiple_of(c * HD, HD), HD)
        scale = 1.0 + columns[0, features, :]
        shift = columns[1, features, :]
        for i in range(PATCH // HD):
            tokens = pl.ds(i * HD, HD)
            value = (xg[features, tokens].astype(F32) - norm_v[0:1, tokens]) * norm_v[1:2, tokens]
            normed[tokens, features] = (value * scale + shift).T.astype(BF16)

    def wait_weights(p):
        view = wqkv.at[p, pl.ds(0, D - ROWS)]
        pltpu.make_async_copy(view, view, rs_w.at[p]).wait()

    def project(p, dst):
        @pl.loop(0, PATCH // Q_STEP)
        def _(i):
            rows = pl.ds(pl.multiple_of(i * Q_STEP, Q_STEP), Q_STEP)
            dst[rows, :] = jnp.dot(normed[rows, :], wqkv[p], preferred_element_type=F32).astype(BF16)

    NT = (((1,), (1,)), ((), ()))
    scaling = HD ** -0.5

    wait_weights(0)
    project(0, q_v)
    load_s.wait()
    patch = patch_ref[0]

    @pl.loop(0, PATCH // Q_STEP)
    def _(i):
        rows = pl.ds(pl.multiple_of(i * Q_STEP, Q_STEP), Q_STEP)
        query = q_v[rows, :]
        scores = []
        for j in range(1, 4):
            keys = stale_v[0, lax.rem(patch + j, 4)]
            scores.append(lax.dot_general(query, keys, NT, preferred_element_type=F32) * scaling)
        scores = jnp.concatenate(scores, axis=1)
        top = jnp.max(scores, axis=1, keepdims=True)
        expo = jnp.exp(scores - top)
        m_stale[rows, :] = jnp.broadcast_to(top, (Q_STEP, HD))
        l_stale[rows, :] = jnp.broadcast_to(jnp.sum(expo, axis=1, keepdims=True), (Q_STEP, HD))
        weights = expo.astype(BF16)
        total = jnp.zeros((Q_STEP, HD), F32)
        for j in range(1, 4):
            values = stale_v[1, lax.rem(patch + j, 4)]
            total += jnp.dot(weights[:, (j - 1) * PATCH : j * PATCH], values, preferred_element_type=F32)
        o_stale[rows, :] = total

    wait_weights(1)
    project(1, k_v)

    @pl.loop(0, PATCH // Q_STEP)
    def _(i):
        rows = pl.ds(pl.multiple_of(i * Q_STEP, Q_STEP), Q_STEP)
        scores = lax.dot_general(q_v[rows, :], k_v[...], NT, preferred_element_type=F32) * scaling
        top = jnp.max(scores, axis=1, keepdims=True)
        expo = jnp.exp(scores - top)
        l_part = jnp.broadcast_to(jnp.sum(expo, axis=1, keepdims=True), (Q_STEP, HD))
        top = jnp.broadcast_to(top, (Q_STEP, HD))
        high = jnp.maximum(top, m_stale[rows, :])
        a_new = jnp.exp(top - high)
        a_old = jnp.exp(m_stale[rows, :] - high)
        inverse = 1.0 / (a_new * l_part + a_old * l_stale[rows, :])
        m_new[rows, :] = a_new * inverse
        o_stale[rows, :] = o_stale[rows, :] * (a_old * inverse)
        p_new[rows, :] = expo.astype(BF16)

    def send_a(slot, c, e):
        rows = pl.ds(pl.multiple_of(c * Q_STEP, Q_STEP), Q_STEP)
        return pltpu.make_async_remote_copy(
            attg.at[slot, rows], attg.at[slot, rows], ss_a.at[e - 1, c], rs_a.at[slot, c],
            device_id=(section, lax.rem(x + e, 4) * 4 + zh), device_id_type=MESH,
        )

    wait_weights(2)
    project(2, v_v)

    @pl.loop(0, CHUNKS)
    def _(c):
        rows = pl.ds(pl.multiple_of(c * Q_STEP, Q_STEP), Q_STEP)
        fresh = jnp.dot(p_new[rows, :], v_v[...], preferred_element_type=F32)
        attg[x, rows, :] = (o_stale[rows, :] + fresh * m_new[rows, :]).astype(BF16)
        for e in range(1, 4):
            send_a(x, c, e).start()

    def along(sign):
        return (section, x * 4 + lax.rem(zh + 4 + sign, 4))

    def remote(src, dst, k, c, sign):
        return pltpu.make_async_remote_copy(
            src, dst, ss_r.at[k, c], rs_r.at[k, c], device_id=along(sign), device_id_type=MESH
        )

    low, high = pl.ds(0, HALF), pl.ds(HALF, HALF)

    def far_up(c):
        return remote(part.at[0, c, low], far_in.at[0, c], 0, c, 1)

    def far_down(c):
        return remote(part.at[0, c, high], far_in.at[1, c], 1, c, -1)

    def plain_up(c):
        return remote(part.at[1, c, high], near_in.at[0, c, high], 2, c, 1)

    def plain_down(c):
        return remote(part.at[2, c, low], near_in.at[1, c, low], 3, c, -1)

    def sum_up(c):
        return remote(part.at[1, c, low], near_in.at[0, c, low], 4, c, 1)

    def sum_down(c):
        return remote(part.at[2, c, high], near_in.at[1, c, high], 5, c, -1)

    for step in (2, 1, 3, 0):
        group = lax.rem(zh + step, 4)
        features = pl.ds(pl.multiple_of(group * SHARE, SHARE), SHARE)
        view = wqkv.at[0, pl.ds(0, 8 * ROWS)]
        pltpu.make_async_copy(view, view, rs_o.at[group]).wait()
        weights = jnp.concatenate([wo[j, features, :] for j in range(4)], axis=1)

        @pl.loop(0, CHUNKS)
        def _(c):
            tokens = pl.ds(pl.multiple_of(c * HD, HD), HD)
            if step == 2:
                for e in range(1, 4):
                    send_a(lax.rem(x + e, 4), c, e).wait_recv()
            attended = jnp.concatenate([attg[j, tokens, :] for j in range(4)], axis=1)
            value = lax.dot_general(weights, attended, NT, preferred_element_type=F32)
            if step == 2:
                part[0, c] = value.astype(BF16)
                far_up(c).start()
                far_down(c).start()
            elif step == 1:
                quarters[1, c] = value
                part[1, c, high, :] = value[HALF:].astype(BF16)
                plain_up(c).start()
            elif step == 3:
                quarters[2, c] = value
                part[2, c, low, :] = value[:HALF].astype(BF16)
                plain_down(c).start()
            else:
                quarters[0, c] = value

    @pl.loop(0, CHUNKS)
    def _(c):
        far_up(c).wait_recv()
        part[1, c, low, :] = (quarters[1, c, low, :] + far_in[0, c].astype(F32)).astype(BF16)
        sum_up(c).start()
        far_down(c).wait_recv()
        part[2, c, high, :] = (quarters[2, c, high, :] + far_in[1, c].astype(F32)).astype(BF16)
        sum_down(c).start()

    def hand(c):
        tokens = pl.ds(pl.multiple_of(c * HD, HD), HD)
        return pltpu.make_async_remote_copy(
            res.at[c], out_ref.at[:, tokens], ss_h.at[c], rs_h.at[c],
            device_id=(lax.rem(section + 1, BLOCKS), t), device_id_type=MESH,
        )

    @pl.loop(0, CHUNKS)
    def _(c):
        for copy in (plain_up, plain_down, sum_up, sum_down):
            copy(c).wait_recv()
        tokens = pl.ds(pl.multiple_of(c * HD, HD), HD)
        mixed = quarters[0, c] + near_in[0, c].astype(F32) + near_in[1, c].astype(F32)
        gate = columns[2, my_features, :]
        res[c] = (xg[my_features, tokens].astype(F32) + gate * mixed).astype(BF16)
        hand(c).start()

    for p in range(4):
        view = wqkv.at[0, pl.ds(0, D - ROWS)]
        pltpu.make_async_copy(view, view, ss_w.at[p]).wait()

    @pl.when(xo != x)
    def _():
        send_o(BLOCKS - 1, ss_own).wait_send()

    for d in range(6):
        send_x(t, (section, t), ss_x.at[d]).wait_send()
    for d in range(9):
        send_x(t, (section, t), ss_f.at[d]).wait_send()

    @pl.loop(0, CHUNKS)
    def _(c):
        for copy in (far_up, far_down, plain_up, plain_down, sum_up, sum_down):
            copy(c).wait_send()
        for e in range(1, 4):
            send_a(x, c, e).wait_send()
        hand(c).wait()


def local(block_weights, modulation, inflow, stale_cache, patch_index, assignment):
    smem = pl.BlockSpec(memory_space=pltpu.SMEM)
    hbm = pl.BlockSpec(memory_space=pltpu.HBM)
    dma = pltpu.SemaphoreType.DMA
    result = pl.pallas_call(
        kernel,
        out_shape=jax.ShapeDtypeStruct((SHARE, PATCH), BF16),
        in_specs=[smem, smem, hbm, hbm, hbm, hbm],
        out_specs=hbm,
        scratch_shapes=[
            pltpu.VMEM((BLOCKS, 4 * ROWS, HD), BF16),
            pltpu.VMEM((3, 1, D), F32),
            pltpu.VMEM((3, D, HD), F32),
            pltpu.VMEM((2, 4, PATCH, HD), BF16),
            pltpu.VMEM((4 * ROWS, 4 * ROWS), BF16),
            pltpu.VMEM((BLOCKS, 4 * ROWS, HD), BF16),
            pltpu.VMEM((3, D, HD), BF16),
            pltpu.VMEM((4, PER_X, HD), BF16),
            pltpu.VMEM((D, PATCH), BF16),
            pltpu.VMEM((PATCH, D), BF16),
            pltpu.VMEM((PATCH, HD), BF16),
            pltpu.VMEM((PATCH, HD), BF16),
            pltpu.VMEM((PATCH, HD), BF16),
            pltpu.VMEM((PATCH, HD), F32),
            pltpu.VMEM((PATCH, HD), F32),
            pltpu.VMEM((PATCH, HD), F32),
            pltpu.VMEM((PATCH, PATCH), BF16),
            pltpu.VMEM((PATCH, HD), F32),
            pltpu.VMEM((4, PATCH, HD), BF16),
            pltpu.VMEM((N_TP, 2, PATCH), F32),
            pltpu.VMEM((8, PATCH), F32),
            pltpu.VMEM((3, CHUNKS, SHARE, HD), F32),
            pltpu.VMEM((3, CHUNKS, SHARE, HD), BF16),
            pltpu.VMEM((2, CHUNKS, HALF, HD), BF16),
            pltpu.VMEM((2, CHUNKS, SHARE, HD), BF16),
            pltpu.VMEM((CHUNKS, SHARE, HD), BF16),
            dma((4,)), dma((4,)), dma((3,)), dma((4,)), dma,
            dma((6,)), dma((N_TP,)), dma((9,)), dma((3, CHUNKS)), dma((4, CHUNKS)), dma((6, CHUNKS)), dma((6, CHUNKS)), dma((CHUNKS,)), dma((CHUNKS,)),
        ],
        compiler_params=pltpu.CompilerParams(
            collective_id=0, has_side_effects=True, vmem_limit_bytes=60 * 2**20
        ),
    )(
        assignment,
        patch_index,
        block_weights.reshape(BLOCKS, 4 * ROWS, HD),
        modulation.transpose(1, 0, 2),
        inflow[0].T,
        stale_cache.reshape(2, 4, PATCH, HD),
    )
    return result.T[None]


def solution(mesh):
    placed = (
        P(None, "section", None, "tp"),
        P("section", None, None),
        P("section", None, "tp"),
        P("section", None, None, "tp"),
        P("section"),
        P(),
    )
    return jax.shard_map(
        local, mesh=mesh, in_specs=placed, out_specs=P("section", None, "tp"), check_vma=False
    )
```

```python
import functools

import jax
import jax.numpy as jnp
from jax import lax
from jax.experimental import pallas as pl
from jax.experimental.pallas import tpu as pltpu
from jax.sharding import PartitionSpec as P

MESH = pl.DeviceIdType.MESH
F32 = jnp.float32
BF16 = jnp.bfloat16

HD = 128
D = 3072
PATCH = 512
SEQ = 2048
BLOCKS = 32
N_TP = 16
ROWS = D // BLOCKS
SHARE = D // N_TP
HALF = SHARE // 2
CHUNKS = PATCH // HD
PER_X = D // 4
Q_STEP = 128


def peer_section(k, section):
    core = lax.rem(section, 2)
    y = lax.rem(section // 2, 8)
    z_lo = section // 16
    turn = k // 4
    flip = 3 - lax.rem(k, 4)
    half = (turn + 1) // 2
    dy = 4 + half * (1 - 2 * lax.rem(turn, 2))
    return (lax.rem(z_lo + flip // 2, 2) * 8 + lax.rem(y + dy, 8)) * 2 + lax.rem(core + lax.rem(flip, 2), 2)


def kernel(
    assign_ref, patch_ref, w_hbm, mod_hbm, x_hbm, stale_hbm, out_ref,
    w_v, mod_v, columns, stale_v, perm_v, send_w, wqkv, wo, xg, normed, q_v, k_v, v_v,
    o_stale, m_stale, l_stale, p_new, m_new, attg, stats, norm_v, quarters, part, far_in, near_in, res,
    sem_loc, ss_w, rs_w, rs_o, ss_own, ss_x, rs_x, ss_f, ss_a, rs_a, ss_r, rs_r, ss_h, rs_h,
):
    section = lax.axis_index("section")
    t = lax.axis_index("tp")
    x = t // 4
    zh = lax.rem(t, 4)
    y = lax.rem(section // 2, 8)
    xo = section // 8

    load_w = pltpu.make_async_copy(w_hbm, w_v, sem_loc.at[0])
    my_features = pl.ds(pl.multiple_of(t * SHARE, SHARE), SHARE)
    load_x = pltpu.make_async_copy(x_hbm, xg.at[my_features], sem_loc.at[1])
    load_s = pltpu.make_async_copy(stale_hbm, stale_v, sem_loc.at[2])
    load_m = pltpu.make_async_copy(mod_hbm, mod_v, sem_loc.at[3])
    load_x.start()
    load_w.start()
    load_m.start()
    load_s.start()

    barrier = pltpu.get_barrier_semaphore()

    def greet(dev):
        pl.semaphore_signal(barrier, inc=1, device_id=dev, device_id_type=MESH)

    @pl.loop(0, BLOCKS - 1)
    def _(k):
        greet((peer_section(k, section), t))

    @pl.loop(0, BLOCKS)
    def _(k):
        greet((x * 8 + k // 4, lax.rem(k, 4) * 4 + zh))

    for d in range(1, 4):
        greet((section, lax.rem(x + d, 4) * 4 + zh))
        greet((section, x * 4 + lax.rem(zh + d, 4)))

    row = lax.broadcasted_iota(jnp.int32, (4 * ROWS, 4 * ROWS), 0)
    col = lax.broadcasted_iota(jnp.int32, (4 * ROWS, 4 * ROWS), 1)
    proj = (row >= ROWS).astype(jnp.int32) + (row >= 2 * ROWS).astype(jnp.int32) + (row >= 3 * ROWS).astype(jnp.int32)
    perm_v[...] = jnp.where(col == (row - proj * ROWS) * 4 + proj, 1.0, 0.0).astype(BF16)

    load_x.wait()
    load_w.wait()

    pl.semaphore_wait(barrier, (BLOCKS - 1) + BLOCKS + 6)

    def send_x(slot, dev, sem):
        rows = pl.ds(pl.multiple_of(slot * SHARE, SHARE), SHARE)
        return pltpu.make_async_remote_copy(
            xg.at[rows], xg.at[rows], sem, rs_x.at[slot], device_id=dev, device_id_type=MESH
        )

    def send_z(d):
        return send_x(t, (section, x * 4 + lax.rem(zh + d, 4)), ss_x.at[d - 1])

    def pass_on(d):
        slot = x * 4 + lax.rem(zh + d, 4)
        send_x(slot, (section, slot), ss_x.at[0]).wait_recv()
        for e in range(1, 4):
            dev = (section, lax.rem(x + e, 4) * 4 + zh)
            send_x(slot, dev, ss_f.at[3 * (d - 1) + e - 1]).start()

    send_z(1).start()
    send_z(3).start()
    send_z(2).start()
    for d in range(1, 4):
        send_x(t, (section, lax.rem(x + d, 4) * 4 + zh), ss_x.at[2 + d]).start()

    def block_of(s):
        owner = jnp.int32(0)
        for b in range(1, BLOCKS):
            owner = jnp.where(assign_ref[b] == s, b, owner)
        return w_v[owner]

    my_rows = pl.ds(pl.multiple_of(section * ROWS, ROWS), ROWS)

    def send_part(k, p):
        return pltpu.make_async_remote_copy(
            send_w.at[k, pl.ds(p * ROWS, ROWS)], wqkv.at[p, my_rows], ss_w.at[p], rs_w.at[p],
            device_id=(peer_section(k, section), t), device_id_type=MESH,
        )

    o_rows = pl.ds(pl.multiple_of(lax.rem(section, 8) * ROWS, ROWS), ROWS)
    o_group = lax.rem(section // 2, 4)

    def send_o(k, sem):
        return pltpu.make_async_remote_copy(
            send_w.at[k, pl.ds(3 * ROWS, ROWS)], wo.at[x, o_rows], sem, rs_o.at[o_group],
            device_id=(peer_section(k, section), xo * 4 + zh), device_id_type=MESH,
        )

    @pl.loop(0, BLOCKS // 4)
    def _(g):
        blocks = jnp.concatenate([block_of(peer_section(4 * g + i, section)) for i in range(4)], axis=1)
        ordered = jnp.dot(perm_v[...], blocks, preferred_element_type=F32).astype(BF16)
        for i in range(4):
            send_w[4 * g + i] = ordered[:, i * HD : (i + 1) * HD]
        for i in range(3):
            send_part(4 * g + i, 0).start()

        @pl.when(g < BLOCKS // 4 - 1)
        def _():
            send_part(4 * g + 3, 0).start()

    for p in range(3):
        wqkv[p, my_rows, :] = send_w[BLOCKS - 1, pl.ds(p * ROWS, ROWS), :]
    @pl.loop(0, BLOCKS - 1)
    def _(k):
        send_part(k, 1).start()

    pass_on(1)
    pass_on(3)

    @pl.loop(0, BLOCKS - 1)
    def _(k):
        send_part(k, 2).start()

    pass_on(2)

    @pl.loop(0, BLOCKS - 1)
    def _(k):
        send_o(k, ss_w.at[3]).start()

    own_o = pltpu.make_async_copy(
        send_w.at[BLOCKS - 1, pl.ds(3 * ROWS, ROWS)], wo.at[x, o_rows], rs_o.at[o_group]
    )

    @pl.when(xo == x)
    def _():
        own_o.start()

    @pl.when(xo != x)
    def _():
        send_o(BLOCKS - 1, ss_own).start()

    load_m.wait()

    @pl.loop(0, D // HD)
    def _(c):
        features = pl.ds(pl.multiple_of(c * HD, HD), HD)
        for p in range(3):
            columns[p, features, :] = jnp.broadcast_to(mod_v[p, :, features], (HD, HD)).T

    def take_stats(slot):
        rows = pl.ds(pl.multiple_of(slot * SHARE, SHARE), SHARE)
        tokens = xg[rows, :].astype(F32)
        mean = jnp.sum(jnp.sum(tokens.reshape(SHARE // 8, 8, PATCH), axis=0), axis=0, keepdims=True) / SHARE
        shifted = tokens - mean
        shifted = shifted * shifted
        moment = jnp.sum(jnp.sum(shifted.reshape(SHARE // 8, 8, PATCH), axis=0), axis=0, keepdims=True)
        stats[slot] = jnp.concatenate([mean, moment], axis=0)

    @pl.loop(0, 4)
    def _(d):
        take_stats(x * 4 + lax.rem(zh + d, 4))

    @pl.loop(0, 12)
    def _(i):
        slot = lax.rem(x + 1 + lax.rem(i, 3), 4) * 4 + lax.rem(zh + i // 3, 4)
        send_x(slot, (section, slot), ss_x.at[0]).wait_recv()
        take_stats(slot)

    means = stats[:, 0, :]
    center = jnp.sum(means, axis=0, keepdims=True) / N_TP
    means = means - center
    moment = jnp.sum(stats[:, 1, :] + SHARE * means * means, axis=0, keepdims=True)
    inverse = lax.rsqrt(moment / D + 1e-06)
    norm_v[0:1, :] = center
    norm_v[1:2, :] = inverse

    @pl.loop(0, D // HD)
    def _(c):
        features = pl.ds(pl.multiple_of(c * HD, HD), HD)
        scale = 1.0 + columns[0, features, :]
        shift = columns[1, features, :]
        for i in range(PATCH // HD):
            tokens = pl.ds(i * HD, HD)
            value = (xg[features, tokens].astype(F32) - norm_v[0:1, tokens]) * norm_v[1:2, tokens]
            normed[tokens, features] = (value * scale + shift).T.astype(BF16)

    def wait_weights(p):
        view = wqkv.at[p, pl.ds(0, D - ROWS)]
        pltpu.make_async_copy(view, view, rs_w.at[p]).wait()

    def project(p, dst):
        @pl.loop(0, PATCH // Q_STEP)
        def _(i):
            rows = pl.ds(pl.multiple_of(i * Q_STEP, Q_STEP), Q_STEP)
            dst[rows, :] = jnp.dot(normed[rows, :], wqkv[p], preferred_element_type=F32).astype(BF16)

    NT = (((1,), (1,)), ((), ()))
    scaling = HD ** -0.5

    wait_weights(0)
    project(0, q_v)
    load_s.wait()
    patch = patch_ref[0]

    @pl.loop(0, PATCH // Q_STEP)
    def _(i):
        rows = pl.ds(pl.multiple_of(i * Q_STEP, Q_STEP), Q_STEP)
        query = q_v[rows, :]
        scores = []
        for j in range(1, 4):
            keys = stale_v[0, lax.rem(patch + j, 4)]
            scores.append(lax.dot_general(query, keys, NT, preferred_element_type=F32) * scaling)
        scores = jnp.concatenate(scores, axis=1)
        top = jnp.max(scores, axis=1, keepdims=True)
        expo = jnp.exp(scores - top)
        m_stale[rows, :] = jnp.broadcast_to(top, (Q_STEP, HD))
        l_stale[rows, :] = jnp.broadcast_to(jnp.sum(expo, axis=1, keepdims=True), (Q_STEP, HD))
        weights = expo.astype(BF16)
        total = jnp.zeros((Q_STEP, HD), F32)
        for j in range(1, 4):
            values = stale_v[1, lax.rem(patch + j, 4)]
            total += jnp.dot(weights[:, (j - 1) * PATCH : j * PATCH], values, preferred_element_type=F32)
        o_stale[rows, :] = total

    wait_weights(1)
    project(1, k_v)

    @pl.loop(0, PATCH // Q_STEP)
    def _(i):
        rows = pl.ds(pl.multiple_of(i * Q_STEP, Q_STEP), Q_STEP)
        scores = lax.dot_general(q_v[rows, :], k_v[...], NT, preferred_element_type=F32) * scaling
        top = jnp.max(scores, axis=1, keepdims=True)
        expo = jnp.exp(scores - top)
        l_part = jnp.broadcast_to(jnp.sum(expo, axis=1, keepdims=True), (Q_STEP, HD))
        top = jnp.broadcast_to(top, (Q_STEP, HD))
        high = jnp.maximum(top, m_stale[rows, :])
        a_new = jnp.exp(top - high)
        a_old = jnp.exp(m_stale[rows, :] - high)
        inverse = 1.0 / (a_new * l_part + a_old * l_stale[rows, :])
        m_new[rows, :] = a_new * inverse
        o_stale[rows, :] = o_stale[rows, :] * (a_old * inverse)
        p_new[rows, :] = expo.astype(BF16)

    def send_a(slot, c, e):
        rows = pl.ds(pl.multiple_of(c * Q_STEP, Q_STEP), Q_STEP)
        return pltpu.make_async_remote_copy(
            attg.at[slot, rows], attg.at[slot, rows], ss_a.at[e - 1, c], rs_a.at[slot, c],
            device_id=(section, lax.rem(x + e, 4) * 4 + zh), device_id_type=MESH,
        )

    wait_weights(2)
    v_v[...] = jnp.dot(normed[...], wqkv[2], preferred_element_type=F32).astype(BF16)

    fresh = jnp.dot(p_new[...], v_v[...], preferred_element_type=F32)
    attg[x] = (o_stale[...] + fresh * m_new[...]).astype(BF16)

    @pl.loop(0, CHUNKS)
    def _(c):
        for e in range(1, 4):
            send_a(x, c, e).start()

    def along(sign):
        return (section, x * 4 + lax.rem(zh + 4 + sign, 4))

    def remote(src, dst, k, c, sign):
        return pltpu.make_async_remote_copy(
            src, dst, ss_r.at[k, c], rs_r.at[k, c], device_id=along(sign), device_id_type=MESH
        )

    low, high = pl.ds(0, HALF), pl.ds(HALF, HALF)

    def far_up(c):
        return remote(part.at[0, c, low], far_in.at[0, c], 0, c, 1)

    def far_down(c):
        return remote(part.at[0, c, high], far_in.at[1, c], 1, c, -1)

    def plain_up(c):
        return remote(part.at[1, c, high], near_in.at[0, c, high], 2, c, 1)

    def plain_down(c):
        return remote(part.at[2, c, low], near_in.at[1, c, low], 3, c, -1)

    def sum_up(c):
        return remote(part.at[1, c, low], near_in.at[0, c, low], 4, c, 1)

    def sum_down(c):
        return remote(part.at[2, c, high], near_in.at[1, c, high], 5, c, -1)

    for step in (2, 1, 3, 0):
        group = lax.rem(zh + step, 4)
        features = pl.ds(pl.multiple_of(group * SHARE, SHARE), SHARE)
        view = wqkv.at[0, pl.ds(0, 8 * ROWS)]
        pltpu.make_async_copy(view, view, rs_o.at[group]).wait()
        weights = jnp.concatenate([wo[j, features, :] for j in range(4)], axis=1)

        @pl.loop(0, CHUNKS)
        def _(c):
            tokens = pl.ds(pl.multiple_of(c * HD, HD), HD)
            if step == 2:
                for e in range(1, 4):
                    send_a(lax.rem(x + e, 4), c, e).wait_recv()
            attended = jnp.concatenate([attg[j, tokens, :] for j in range(4)], axis=1)
            value = lax.dot_general(weights, attended, NT, preferred_element_type=F32)
            if step == 2:
                part[0, c] = value.astype(BF16)
                far_up(c).start()
                far_down(c).start()
            elif step == 1:
                quarters[1, c] = value
                part[1, c, high, :] = value[HALF:].astype(BF16)
                plain_up(c).start()
            elif step == 3:
                quarters[2, c] = value
                part[2, c, low, :] = value[:HALF].astype(BF16)
                plain_down(c).start()
            else:
                quarters[0, c] = value

    @pl.loop(0, CHUNKS)
    def _(c):
        far_up(c).wait_recv()
        part[1, c, low, :] = (quarters[1, c, low, :] + far_in[0, c].astype(F32)).astype(BF16)
        sum_up(c).start()
        far_down(c).wait_recv()
        part[2, c, high, :] = (quarters[2, c, high, :] + far_in[1, c].astype(F32)).astype(BF16)
        sum_down(c).start()

    def hand(c):
        tokens = pl.ds(pl.multiple_of(c * HD, HD), HD)
        return pltpu.make_async_remote_copy(
            res.at[c], out_ref.at[:, tokens], ss_h.at[c], rs_h.at[c],
            device_id=(lax.rem(section + 1, BLOCKS), t), device_id_type=MESH,
        )

    @pl.loop(0, CHUNKS)
    def _(c):
        for copy in (plain_up, plain_down, sum_up, sum_down):
            copy(c).wait_recv()
        tokens = pl.ds(pl.multiple_of(c * HD, HD), HD)
        mixed = quarters[0, c] + near_in[0, c].astype(F32) + near_in[1, c].astype(F32)
        gate = columns[2, my_features, :]
        res[c] = (xg[my_features, tokens].astype(F32) + gate * mixed).astype(BF16)
        hand(c).start()

    for p in range(4):
        view = wqkv.at[0, pl.ds(0, D - ROWS)]
        pltpu.make_async_copy(view, view, ss_w.at[p]).wait()

    @pl.when(xo != x)
    def _():
        send_o(BLOCKS - 1, ss_own).wait_send()

    for d in range(6):
        send_x(t, (section, t), ss_x.at[d]).wait_send()
    for d in range(9):
        send_x(t, (section, t), ss_f.at[d]).wait_send()

    @pl.loop(0, CHUNKS)
    def _(c):
        for copy in (far_up, far_down, plain_up, plain_down, sum_up, sum_down):
            copy(c).wait_send()
        for e in range(1, 4):
            send_a(x, c, e).wait_send()
        hand(c).wait()


def local(block_weights, modulation, inflow, stale_cache, patch_index, assignment):
    smem = pl.BlockSpec(memory_space=pltpu.SMEM)
    hbm = pl.BlockSpec(memory_space=pltpu.HBM)
    dma = pltpu.SemaphoreType.DMA
    result = pl.pallas_call(
        kernel,
        out_shape=jax.ShapeDtypeStruct((SHARE, PATCH), BF16),
        in_specs=[smem, smem, hbm, hbm, hbm, hbm],
        out_specs=hbm,
        scratch_shapes=[
            pltpu.VMEM((BLOCKS, 4 * ROWS, HD), BF16),
            pltpu.VMEM((3, 1, D), F32),
            pltpu.VMEM((3, D, HD), F32),
            pltpu.VMEM((2, 4, PATCH, HD), BF16),
            pltpu.VMEM((4 * ROWS, 4 * ROWS), BF16),
            pltpu.VMEM((BLOCKS, 4 * ROWS, HD), BF16),
            pltpu.VMEM((3, D, HD), BF16),
            pltpu.VMEM((4, PER_X, HD), BF16),
            pltpu.VMEM((D, PATCH), BF16),
            pltpu.VMEM((PATCH, D), BF16),
            pltpu.VMEM((PATCH, HD), BF16),
            pltpu.VMEM((PATCH, HD), BF16),
            pltpu.VMEM((PATCH, HD), BF16),
            pltpu.VMEM((PATCH, HD), F32),
            pltpu.VMEM((PATCH, HD), F32),
            pltpu.VMEM((PATCH, HD), F32),
            pltpu.VMEM((PATCH, PATCH), BF16),
            pltpu.VMEM((PATCH, HD), F32),
            pltpu.VMEM((4, PATCH, HD), BF16),
            pltpu.VMEM((N_TP, 2, PATCH), F32),
            pltpu.VMEM((8, PATCH), F32),
            pltpu.VMEM((3, CHUNKS, SHARE, HD), F32),
            pltpu.VMEM((3, CHUNKS, SHARE, HD), BF16),
            pltpu.VMEM((2, CHUNKS, HALF, HD), BF16),
            pltpu.VMEM((2, CHUNKS, SHARE, HD), BF16),
            pltpu.VMEM((CHUNKS, SHARE, HD), BF16),
            dma((4,)), dma((4,)), dma((3,)), dma((4,)), dma,
            dma((6,)), dma((N_TP,)), dma((9,)), dma((3, CHUNKS)), dma((4, CHUNKS)), dma((6, CHUNKS)), dma((6, CHUNKS)), dma((CHUNKS,)), dma((CHUNKS,)),
        ],
        compiler_params=pltpu.CompilerParams(
            collective_id=0, has_side_effects=True, vmem_limit_bytes=60 * 2**20
        ),
    )(
        assignment,
        patch_index,
        block_weights.reshape(BLOCKS, 4 * ROWS, HD),
        modulation.transpose(1, 0, 2),
        inflow[0].T,
        stale_cache.reshape(2, 4, PATCH, HD),
    )
    return result.T[None]


def solution(mesh):
    placed = (
        P(None, "section", None, "tp"),
        P("section", None, None),
        P("section", None, "tp"),
        P("section", None, None, "tp"),
        P("section"),
        P(),
    )
    return jax.shard_map(
        local, mesh=mesh, in_specs=placed, out_specs=P("section", None, "tp"), check_vma=False
    )
```
